32 devices in a mesh: clip: 4 (over y, x), tm: 8 (over z, core).
Axes of the slice: x: 2, y: 2, z: 4, core: 2. Of those that a mesh axis runs over, the one named last changes fastest.
Arguments:
- clip_in: bfloat16 [8, 32, 14, 14, 1024], P('clip', 'tm'), may hold values from -6 to 6
- cotangent: bfloat16 [8, 16, 7, 7, 2048], P('clip', 'tm'), may hold values from -6 to 6
- frame_count: int32 [8], replicated, may hold values from 2 to 4, as said below
- clip_count: int32 [4], P('clip'), may hold values from 1 to 2, as said below
- narrow_a: bfloat16 [1024, 256], replicated, may hold values from -0.1875 to 0.1875
- narrow_gain_a: float32 [256], replicated, may hold values from 0.5 to 1.5
- narrow_bias_a: float32 [256], replicated, may hold values from -0.5 to 0.5
- mixing_a: bfloat16 [256, 256], replicated, may hold values from -0.375 to 0.375
- depthwise_a: bfloat16 [256, 27], replicated, may hold values from -1.25 to 1.25
- depth_gain_a: float32 [256], replicated, may hold values from 0.5 to 1.5
- depth_bias_a: float32 [256], replicated, may hold values from -0.5 to 0.5
- widen_a: bfloat16 [256, 1024], replicated, may hold values from -0.375 to 0.375
- widen_gain_a: float32 [1024], replicated, may hold values from 0.5 to 1.5
- widen_bias_a: float32 [1024], replicated, may hold values from -0.5 to 0.5
- narrow_b: bfloat16 [1024, 512], replicated, may hold values from -0.1875 to 0.1875
- narrow_gain_b: float32 [512], replicated, may hold values from 0.5 to 1.5
- narrow_bias_b: float32 [512], replicated, may hold values from -0.5 to 0.5
- mixing_b: bfloat16 [512, 512], replicated, may hold values from -0.25 to 0.25
- depthwise_b: bfloat16 [512, 27], replicated, may hold values from -1.25 to 1.25
- depth_gain_b: float32 [512], replicated, may hold values from 0.5 to 1.5
- depth_bias_b: float32 [512], replicated, may hold values from -0.5 to 0.5
- widen_b: bfloat16 [512, 2048], replicated, may hold values from -0.25 to 0.25
- widen_gain_b: float32 [2048], replicated, may hold values from 0.5 to 1.5
- widen_bias_b: float32 [2048], replicated, may hold values from -0.5 to 0.5
- shortcut_b: bfloat16 [1024, 2048], replicated, may hold values from -0.1875 to 0.1875
- shortcut_gain_b: float32 [2048], replicated, may hold values from 0.5 to 1.5
- shortcut_bias_b: float32 [2048], replicated, may hold values from -0.5 to 0.5
Outputs:
- block_out: bfloat16 [8, 16, 7, 7, 2048], P('clip', 'tm')
- input_grad: bfloat16 [8, 32, 14, 14, 1024], P('clip', 'tm')
- grad_narrow_a: float32 [1024, 256], P('tm')
- grad_narrow_gain_a: float32 [256], replicated
- grad_narrow_bias_a: float32 [256], replicated
- grad_mixing_a: float32 [256, 256], P('tm')
- grad_depthwise_a: float32 [256, 27], P('tm')
- grad_depth_gain_a: float32 [256], replicated
- grad_depth_bias_a: float32 [256], replicated
- grad_widen_a: float32 [256, 1024], P('tm')
- grad_widen_gain_a: float32 [1024], replicated
- grad_widen_bias_a: float32 [1024], replicated
- grad_narrow_b: float32 [1024, 512], P('tm')
- grad_narrow_gain_b: float32 [512], replicated
- grad_narrow_bias_b: float32 [512], replicated
- grad_mixing_b: float32 [512, 512], P('tm')
- grad_depthwise_b: float32 [512, 27], P('tm')
- grad_depth_gain_b: float32 [512], replicated
- grad_depth_bias_b: float32 [512], replicated
- grad_widen_b: float32 [512, 2048], P('tm')
- grad_widen_gain_b: float32 [2048], replicated
- grad_widen_bias_b: float32 [2048], replicated
- grad_shortcut_b: float32 [1024, 2048], P('tm')
- grad_shortcut_gain_b: float32 [2048], replicated
- grad_shortcut_bias_b: float32 [2048], replicated
The draws below stay inside these ranges and needn't reach their ends.
Inputs may be any that keep to these rules, and one draw needn't show every extreme that they name: Index i of tm holds frame_count[i] consecutive frames of every clip, in order of i; the counts of indices 2 k and 2 k + 1 sum to 6; some index holds exactly 4 in every draw. Clip slots 0 .. clip_count[k] - 1 of clip index k are live; some index has all 2 live in every draw.
All inputs are finite; a program needn't handle non-finite values.
Results may differ from the reference program's by a relative error of at most 0.02.
Values may be sent and summed in bfloat16 or wider, within the bound.
A program may use at most 384 MiB of HBM per device.

```python
import jax
import jax.numpy as jnp
from jax import lax

IN_CH = 1024
MID_A = 256
MID_B = 512
OUT_CH = 2048
HEIGHT = 14
WIDTH = 14
CLIPS_DEV = 2
F_DEV = 3
CAP = 4
HALF_CAP = 2
FRAMES = 24
OUT_FRAMES = 12
CLIPS = 8
N_CLIP = 4
N_TM = 8


def draw_frame_count(key, part):
    key = jax.random.fold_in(key, 11)
    key_shift, key_pick, key_sign = jax.random.split(key, 3)
    couples = N_TM // 2
    largest = F_DEV - 2
    displace = jax.random.randint(key_shift, (couples,), -largest, largest + 1)
    chosen = jax.random.randint(key_pick, (), 0, couples)
    direction = 2 * jax.random.randint(key_sign, (), 0, 2) - 1
    displace = jnp.where(jnp.arange(couples) == chosen, direction * largest, displace)
    return jnp.stack([F_DEV + displace, F_DEV - displace], axis=1).reshape(N_TM).astype(jnp.int32)


def draw_clip_count(key, part):
    key = jax.random.fold_in(key, 23)
    key_count, key_pick = jax.random.split(key)
    counts = jax.random.randint(key_count, (N_CLIP,), 1, CLIPS_DEV + 1)
    chosen = jax.random.randint(key_pick, (), 0, N_CLIP)
    return jnp.where(jnp.arange(N_CLIP) == chosen, CLIPS_DEV, counts).astype(jnp.int32)


def level_of(key, shape, cuts, least, top_value):
    def one(axis_at, parts):
        draws = jax.random.uniform(jax.random.fold_in(jax.random.fold_in(key, 6), axis_at), (parts,), jnp.float32, least / len(cuts), top_value / len(cuts))
        return jnp.repeat(jnp.exp(draws), shape[axis_at] // parts).reshape((-1,) + (1,) * (len(shape) - axis_at - 1))

    level = one(*cuts[0])
    for cut in cuts[1:]:
        level = level * one(*cut)
    return level


def bell_draw(rng, shape, width, bound, pieces=(), held_as=jnp.bfloat16):
    loudness = level_of(rng, shape, pieces, -0.22, 0.18) if pieces else 1.0
    values = jax.random.normal(rng, shape, jnp.float32) * width * loudness
    return jnp.minimum(jnp.maximum(values, -bound), bound).astype(held_as)


def setup_inputs(seed: int = 0) -> dict:
    streams_of = jax.random.split(jax.random.key(seed), 28)
    clip_in = bell_draw(streams_of[0], (CLIPS, N_TM * CAP, HEIGHT, WIDTH, IN_CH), 1.0, 6.0, ((0, 4), (1, 8)))
    cotangent = bell_draw(streams_of[1], (CLIPS, N_TM * HALF_CAP, HEIGHT // 2, WIDTH // 2, OUT_CH), 1.0, 6.0, ((0, 4), (1, 8)))
    frame_count = draw_frame_count(jax.random.fold_in(streams_of[27], 71), 0)
    clip_count = draw_clip_count(jax.random.fold_in(streams_of[27], 71), 0)
    narrow_a = bell_draw(streams_of[4], (IN_CH, MID_A), IN_CH ** -0.5, 0.1875)
    narrow_gain_a = jnp.clip(1.0 + 0.1 * jax.random.normal(streams_of[5], (MID_A,), jnp.float32), 0.5, 1.5)
    narrow_bias_a = jnp.clip(jax.random.uniform(streams_of[6], (MID_A,), jnp.float32, -0.5, 0.5), -0.5, 0.5)
    mixing_a = bell_draw(streams_of[7], (MID_A, MID_A), MID_A ** -0.5, 0.375)
    depthwise_a = bell_draw(streams_of[8], (MID_A, 27), 27 ** -0.5, 1.25)
    depth_gain_a = jnp.clip(1.0 + 0.1 * jax.random.normal(streams_of[9], (MID_A,), jnp.float32), 0.5, 1.5)
    depth_bias_a = jnp.clip(jax.random.uniform(streams_of[10], (MID_A,), jnp.float32, -0.5, 0.5), -0.5, 0.5)
    widen_a = bell_draw(streams_of[11], (MID_A, IN_CH), MID_A ** -0.5, 0.375)
    widen_gain_a = jnp.clip(1.0 + 0.1 * jax.random.normal(streams_of[12], (IN_CH,), jnp.float32), 0.5, 1.5)
    widen_bias_a = jnp.clip(jax.random.uniform(streams_of[13], (IN_CH,), jnp.float32, -0.5, 0.5), -0.5, 0.5)
    narrow_b = bell_draw(streams_of[14], (IN_CH, MID_B), IN_CH ** -0.5, 0.1875)
    narrow_gain_b = jnp.clip(1.0 + 0.1 * jax.random.normal(streams_of[15], (MID_B,), jnp.float32), 0.5, 1.5)
    narrow_bias_b = jnp.clip(jax.random.uniform(streams_of[16], (MID_B,), jnp.float32, -0.5, 0.5), -0.5, 0.5)
    mixing_b = bell_draw(streams_of[17], (MID_B, MID_B), MID_B ** -0.5, 0.25)
    depthwise_b = bell_draw(streams_of[18], (MID_B, 27), 27 ** -0.5, 1.25)
    depth_gain_b = jnp.clip(1.0 + 0.1 * jax.random.normal(streams_of[19], (MID_B,), jnp.float32), 0.5, 1.5)
    depth_bias_b = jnp.clip(jax.random.uniform(streams_of[20], (MID_B,), jnp.float32, -0.5, 0.5), -0.5, 0.5)
    widen_b = bell_draw(streams_of[21], (MID_B, OUT_CH), MID_B ** -0.5, 0.25)
    widen_gain_b = jnp.clip(1.0 + 0.1 * jax.random.normal(streams_of[22], (OUT_CH,), jnp.float32), 0.5, 1.5)
    widen_bias_b = jnp.clip(jax.random.uniform(streams_of[23], (OUT_CH,), jnp.float32, -0.5, 0.5), -0.5, 0.5)
    shortcut_b = bell_draw(streams_of[24], (IN_CH, OUT_CH), IN_CH ** -0.5, 0.1875)
    shortcut_gain_b = jnp.clip(1.0 + 0.1 * jax.random.normal(streams_of[25], (OUT_CH,), jnp.float32), 0.5, 1.5)
    shortcut_bias_b = jnp.clip(jax.random.uniform(streams_of[26], (OUT_CH,), jnp.float32, -0.5, 0.5), -0.5, 0.5)
    return dict(clip_in=clip_in, cotangent=cotangent, frame_count=frame_count, clip_count=clip_count, narrow_a=narrow_a, narrow_gain_a=narrow_gain_a, narrow_bias_a=narrow_bias_a, mixing_a=mixing_a, depthwise_a=depthwise_a, depth_gain_a=depth_gain_a, depth_bias_a=depth_bias_a, widen_a=widen_a, widen_gain_a=widen_gain_a, widen_bias_a=widen_bias_a, narrow_b=narrow_b, narrow_gain_b=narrow_gain_b, narrow_bias_b=narrow_bias_b, mixing_b=mixing_b, depthwise_b=depthwise_b, depth_gain_b=depth_gain_b, depth_bias_b=depth_bias_b, widen_b=widen_b, widen_gain_b=widen_gain_b, widen_bias_b=widen_bias_b, shortcut_b=shortcut_b, shortcut_gain_b=shortcut_gain_b, shortcut_bias_b=shortcut_bias_b)


epsilon = 1e-05
highest = lax.Precision.HIGHEST

@jax.custom_vjp
def low(v):
    return lax.optimization_barrier(v.astype(jnp.bfloat16)).astype(jnp.float32)

@jax.custom_vjp
def low_back(v):
    return v

def low_keep(v):
    return (low(v), None)

def low_pass(kept, grad):
    return (grad,)

def back_keep(v):
    return (v, None)

def back_low(kept, grad):
    return (low(grad),)
low.defvjp(low_keep, low_pass)
low_back.defvjp(back_keep, back_low)

def dense(value, weight):
    return jnp.einsum('nthwc,cd->nthwd', value, weight, precision=highest)

def batch_norm(value, live, voxels, gain, bias):
    centre = lax.optimization_barrier(jnp.sum(value * live, axis=(0, 1, 2, 3))) / voxels
    spread = lax.optimization_barrier(jnp.sum(value * live * value, axis=(0, 1, 2, 3))) / voxels - centre * centre
    return (value - centre) * lax.rsqrt(spread + epsilon) * gain + bias

def depth_conv(value, kernel, stride):
    spaced = jnp.pad(value, ((0, 0), (1, 1), (1, 1), (1, 1), (0, 0)))
    out_depth = (value.shape[1] - 1) // stride + 1
    out_rows = (value.shape[2] - 1) // stride + 1
    out_cols = (value.shape[3] - 1) // stride + 1
    summed = jnp.zeros((value.shape[0], out_depth, out_rows, out_cols, value.shape[4]), jnp.float32)
    for offset in range(27):
        depth_tap, height_tap, across_tap = (offset // 9, offset // 3 % 3, offset % 3)
        window = spaced[:, depth_tap:depth_tap + stride * (out_depth - 1) + 1:stride, height_tap:height_tap + stride * (out_rows - 1) + 1:stride, across_tap:across_tap + stride * (out_cols - 1) + 1:stride]
        summed = summed + window * kernel[:, offset]
    return summed

def first_block(inputs, live, count_full, params):
    narrow, narrow_gain, narrow_bias, mixing, kernel, depth_gain, depth_bias, widen, widen_gain, widen_bias = params
    reduced = low_back(dense(inputs, narrow))
    hidden = low(jax.nn.silu(batch_norm(reduced, live, count_full, narrow_gain, narrow_bias)) * live)
    mixed = low_back(low(dense(hidden, mixing)))
    filtered = depth_conv(mixed, kernel, 1)
    second = low(jax.nn.silu(batch_norm(filtered, live, count_full, depth_gain, depth_bias)) * live)
    widened = low_back(dense(second, widen))
    return jax.nn.silu(batch_norm(widened, live, count_full, widen_gain, widen_bias) + inputs) * live

def second_block(inputs, live, count_full, count_half, params):
    narrow, narrow_gain, narrow_bias, mixing, kernel, depth_gain, depth_bias, widen, widen_gain, widen_bias, shortcut, shortcut_gain, shortcut_bias = params
    rounded = low(inputs)
    reduced = low_back(dense(rounded, narrow))
    hidden = low(jax.nn.silu(batch_norm(reduced, live, count_full, narrow_gain, narrow_bias)) * live)
    mixed = low_back(low(dense(hidden, mixing)))
    filtered = depth_conv(mixed, kernel, 2)
    second = low(jax.nn.silu(batch_norm(filtered, live, count_half, depth_gain, depth_bias)) * live)
    widened = low_back(dense(second, widen))
    skipped = low_back(dense(rounded[:, ::2, ::2, ::2], shortcut))
    joined = batch_norm(widened, live, count_half, widen_gain, widen_bias) + batch_norm(skipped, live, count_half, shortcut_gain, shortcut_bias)
    return jax.nn.silu(joined) * live

def reference(clip_in, cotangent, frame_count, clip_count, narrow_a, narrow_gain_a, narrow_bias_a, mixing_a, depthwise_a, depth_gain_a, depth_bias_a, widen_a, widen_gain_a, widen_bias_a, narrow_b, narrow_gain_b, narrow_bias_b, mixing_b, depthwise_b, depth_gain_b, depth_bias_b, widen_b, widen_gain_b, widen_bias_b, shortcut_b, shortcut_gain_b, shortcut_bias_b):
    counts = frame_count.astype(jnp.int32)
    starts = (jnp.cumsum(counts) - counts).astype(jnp.int32)
    frame_ids = jnp.arange(FRAMES, dtype=jnp.int32)
    owner = (lax.optimization_barrier(jnp.sum((starts[None, :] <= frame_ids[:, None]).astype(jnp.int32), axis=1)) - 1).astype(jnp.int32)
    source_slot = (owner * CAP + frame_ids - starts[owner]).astype(jnp.int32)
    parity = (starts % 2).astype(jnp.int32)
    out_counts = ((counts + 1 - parity) // 2).astype(jnp.int32)
    places = jnp.arange(HALF_CAP, dtype=jnp.int32)
    target = jnp.minimum((starts[:, None] + 1) // 2 + places[None, :], OUT_FRAMES - 1).reshape(-1).astype(jnp.int32)
    valid = (places[None, :] < out_counts[:, None]).astype(jnp.float32).reshape(1, -1, 1, 1, 1)
    clip_ids = jnp.arange(CLIPS, dtype=jnp.int32)
    live = (clip_ids % CLIPS_DEV < clip_count[clip_ids // CLIPS_DEV]).astype(jnp.float32).reshape(-1, 1, 1, 1, 1)
    count_full = jnp.sum(live) * float(FRAMES * HEIGHT * WIDTH)
    count_half = jnp.sum(live) * float(OUT_FRAMES * (HEIGHT // 2) * (WIDTH // 2))
    first_params = tuple((item.astype(jnp.float32) for item in (narrow_a, narrow_gain_a, narrow_bias_a, mixing_a, depthwise_a, depth_gain_a, depth_bias_a, widen_a, widen_gain_a, widen_bias_a)))
    second_params = tuple((item.astype(jnp.float32) for item in (narrow_b, narrow_gain_b, narrow_bias_b, mixing_b, depthwise_b, depth_gain_b, depth_bias_b, widen_b, widen_gain_b, widen_bias_b, shortcut_b, shortcut_gain_b, shortcut_bias_b)))

    def forward(inputs, params_one, params_two):
        ordered = jnp.take(inputs, source_slot, axis=1)
        middle = jax.checkpoint(first_block)(ordered, live, count_full, params_one)
        result = second_block(middle, live, count_full, count_half, params_two)
        return jnp.take(result, target, axis=1) * valid
    output, pullback = jax.vjp(forward, clip_in.astype(jnp.float32), first_params, second_params)
    grad_input, grad_one, grad_two = pullback(cotangent.astype(jnp.float32))
    return (output.astype(jnp.bfloat16), grad_input.astype(jnp.bfloat16), grad_one[0], grad_one[1], grad_one[2], grad_one[3], grad_one[4], grad_one[5], grad_one[6], grad_one[7], grad_one[8], grad_one[9], grad_two[0], grad_two[1], grad_two[2], grad_two[3], grad_two[4], grad_two[5], grad_two[6], grad_two[7], grad_two[8], grad_two[9], grad_two[10], grad_two[11], grad_two[12])
```

```python
import functools

import jax
import jax.numpy as jnp
from jax import lax
from jax.experimental import pallas as pl
from jax.experimental.pallas import tpu as pltpu
from jax.sharding import PartitionSpec as P

epsilon = 1e-05
LANES = 128
MESH = pl.DeviceIdType.MESH
F32 = jnp.float32
BF16 = jnp.bfloat16

NORMS = ("na", "da", "wa", "nb", "db", "wb", "sb")


HALO = (("dva", "dva"), ("hs2", "hr2"), ("dz2", "hr3"), ("hs2", "hr2"))


class Refs:
    pass


def logistic(z):
    return 0.5 * jnp.tanh(0.5 * z) + 0.5


def silu(z):
    return z * logistic(z)


def slope(z):
    q = logistic(z)
    return q * (1.0 + z * (1.0 - q))


def dot(x, w):
    return jnp.dot(x, w, preferred_element_type=F32)


def dot_bt(x, w):
    return lax.dot_general(x, w, (((1,), (1,)), ((), ())), preferred_element_type=F32)


def dot_at(x, y):
    return lax.dot_general(x, y, (((0,), (0,)), ((), ())), preferred_element_type=F32)


def rows8(v):
    return jnp.sum(v.reshape(v.shape[0] // 8, 8, v.shape[1]), axis=0)


def tile_lanes(v, width):
    if width == v.shape[1]:
        return v
    return jnp.concatenate([v] * (width // v.shape[1]), axis=1)


class Dims:
    def __init__(self, mesh, clip_in, cotangent, ca, cb):
        self.nc = mesh.shape["clip"]
        self.nt = mesh.shape["tm"]
        self.phases = [("tm", 1, self.nt)] if self.nt <= 8 else [("tm", 1, 8), ("tm", 8, self.nt // 8)]
        self.phases.append(("clip", 1, self.nc))
        self.n, self.t, self.h, self.w, self.c0 = clip_in
        self.ca, self.cb = ca, cb
        self.co = cotangent[-1]
        self.wp = -(-(self.w + 1) // 16) * 16
        self.f = self.n * self.t
        self.fr = self.h * self.wp
        self.er = (self.h + 2) * self.wp
        self.slots = self.t + 2
        self.t2, self.h2, self.w2 = self.t // 2, self.h // 2, self.w // 2
        self.wh = self.wp // 2
        self.f2 = self.n * self.t2
        self.hr = self.h2 * self.wh
        self.r2 = self.f2 * self.hr
        self.ur = (self.h2 + 1) * self.wp


def messages(d):
    return dict(
        na=(3, d.ca), da=(2, d.ca), wa=(2, d.c0), nb=(2, d.cb), sk=(2, d.co), db=(2, d.cb),
        wb=(2, d.co), gz=(3, d.co), gdb=(2, d.cb), gnb=(2, d.cb), gwa=(2, d.c0), gda=(2, d.ca),
        gna=(2, d.ca),
    )


def scratch_of(d):
    V = pltpu.VMEM
    DM = pltpu.SemaphoreType.DMA
    s = dict(
        raw=V((2, d.h, d.w, d.c0), BF16),
        x=V((d.f, d.h, d.wp, d.c0), BF16),
        a1=V((d.f, d.fr, d.ca), F32),
        h1=V((d.f, d.fr, d.ca), BF16),
        v1=V((d.n * d.slots, d.er, d.ca), BF16),
        d1=V((d.f, d.fr, d.ca), F32),
        h2=V((d.f, d.fr, d.ca), BF16),
        a3=V((d.f, d.fr, d.c0), BF16),
        y1=V((d.f, d.fr, d.c0), BF16),
        b1=V((d.f, d.fr, d.cb), F32),
        g1=V((d.f, d.fr, d.cb), BF16),
        v2=V((d.n * d.slots, d.er, d.cb), BF16),
        d2=V((d.f2, d.hr, d.cb), F32),
        g2=V((d.r2, d.cb), BF16),
        e=V((d.f2, d.hr, d.c0), F32),
        eb=V((d.r2, d.c0), BF16),
        b3s=V((2 * (d.co // d.cb), d.r2, d.cb), F32),
        dz2=V((d.co // d.cb, d.r2, d.cb), F32),
        db3=V((d.r2, d.co), BF16),
        ds=V((d.r2, d.co), BF16),
        u=V((d.n * d.slots, d.er, d.ca), F32),
        dvb=V((d.f, d.fr, d.cb), BF16),
        dz1=V((d.f, d.fr, d.c0), BF16),
        dva=V((max(d.f, 4 * d.n), d.fr, d.ca), BF16),
        cot=V((d.n, d.t2, d.h2, d.w2, d.co), BF16),
        acc=V((3, 8, d.co), F32),
        inv=V((1, d.co), F32),
        kta=V((32, d.ca), F32),
        ktb=V((32, d.cb), F32),
        vec=V((16, d.co), F32),
        gka=V((32, d.ca), F32),
        gkb=V((32, d.cb), F32),
        par=V((len(NORMS), 8, d.co), F32),
        hs2=V((2, d.n, d.fr, d.cb), BF16),
        hr2=V((2, d.n, d.fr, d.cb), BF16),
        hr3=V((2, 2, d.n * d.hr, d.cb), F32),
        hsend=DM((4, 2)),
        hrecv=DM((4, 2)),
        w_na=V((d.c0, d.ca), BF16),
        w_ma=V((d.ca, d.ca), BF16),
        w_wa=V((d.ca, d.c0), BF16),
        w_nb=V((d.c0, d.cb), BF16),
        w_mb=V((d.cb, d.cb), BF16),
        w_wb=V((d.cb, d.co), BF16),
        w_sb=V((d.c0, d.co), BF16),
        small=V((16, d.co), F32),
        wsem=DM((16,)),
        xsem=DM((2,)),
        osem=DM((16,)),
        isem=DM((2,)),
    )
    for name, (k, c) in messages(d).items():
        for p, (_, _, size) in enumerate(d.phases):
            s[f"ms{p}_{name}"] = V((k, c), F32)
            s[f"ml{p}_{name}"] = V((size, k, c), F32)
        s["mq_" + name] = DM((len(d.phases), 2))
    return s


INPUTS = (
    "clip_in", "cotangent", "frame_count", "clip_count", "i_na", "i_ma", "i_wa", "i_nb", "i_mb",
    "i_wb", "i_sb", "i_kta", "i_ktb", "i_vec",
)
OUTPUTS = (
    "block_out", "input_grad", "o_small", "o_gka", "o_gkb", "o_na", "o_ma", "o_wa", "o_nb", "o_mb",
    "o_wb", "o_sb",
)
WEIGHTS = ("na", "ma", "wa", "nb", "mb", "wb", "sb")


def kernel(d, names, *refs):
    r = Refs()
    for name, ref in zip(names, refs):
        setattr(r, name, ref)
    clip = lax.axis_index("clip")
    tm = lax.axis_index("tm")
    msgs = messages(d)

    def weight_copy(i):
        name = WEIGHTS[i]
        return pltpu.make_async_copy(
            getattr(r, "i_" + name), getattr(r, "w_" + name), r.wsem.at[i]
        )

    def frame_copy(f, slot):
        return pltpu.make_async_copy(r.clip_in.at[f // d.t, f % d.t], r.raw.at[slot], r.xsem.at[slot])

    frame_copy(0, 0).start()
    weight_copy(0).start()
    frame_copy(1, 1).start()
    for i, (src, dst) in enumerate(
        ((r.i_kta, r.kta), (r.i_ktb, r.ktb), (r.i_vec, r.vec), (r.cotangent, r.cot))
    ):
        pltpu.make_async_copy(src, dst, r.wsem.at[8 + i]).start()
    for i in range(1, len(WEIGHTS)):
        weight_copy(i).start()

    barrier = pltpu.get_barrier_semaphore()

    def place(p):
        axis, stride, size = d.phases[p]
        return lax.rem((clip if axis == "clip" else tm) // stride, size)

    def peer(p, k):
        axis, stride, size = d.phases[p]
        shift = (lax.rem(place(p) + k, size) - place(p)) * stride
        return (clip + shift, tm) if axis == "clip" else (clip, tm + shift)

    for p in range(len(d.phases)):
        @pl.loop(1, d.phases[p][2])
        def _(k):
            pl.semaphore_signal(barrier, 1, device_id=peer(p, k), device_id_type=MESH)

    frames = jnp.clip(r.frame_count[tm], 2, d.t)
    start = lax.fori_loop(
        0, d.nt, lambda i, s: s + jnp.where(i < tm, r.frame_count[i], 0), jnp.int32(0)
    )
    parity = start & 1
    out_frames = jnp.clip((frames + 1 - parity) // 2, 1, d.t2)
    live = r.clip_count[0]

    def one(cond):
        return jnp.where(cond, 1.0, 0.0).astype(F32)

    def mask_f(f):
        return one((lax.rem(f, d.t) < frames) & (f // d.t < live))

    def mask_o(i):
        return one((lax.rem(i, d.t2) < out_frames) & (i // d.t2 < live))

    has_prev = one(tm > 0)
    has_next = one(tm < d.nt - 1)

    full_cols = one(lax.rem(lax.broadcasted_iota(jnp.int32, (d.fr, LANES), 0), d.wp) < d.w)
    half_cols = one(lax.rem(lax.broadcasted_iota(jnp.int32, (d.hr, LANES), 0), d.wh) < d.w2)
    row_cols = one(lax.broadcasted_iota(jnp.int32, (d.wp, LANES), 0) < d.w)

    last = len(d.phases) - 1

    def ar_send(name, p, value):
        src, slots = getattr(r, f"ms{p}_{name}"), getattr(r, f"ml{p}_{name}")
        q = getattr(r, "mq_" + name)
        src[...] = value

        @pl.loop(1, d.phases[p][2])
        def _(k):
            pltpu.make_async_remote_copy(
                src, slots.at[place(p)], q.at[p, 0], q.at[p, 1], device_id=peer(p, k),
                device_id_type=MESH,
            ).start()

        slots[place(p)] = value

    def ar_wait(name, p, which):
        part = getattr(r, f"ml{p}_{name}").at[pl.ds(0, d.phases[p][2] - 1)]
        pltpu.make_async_copy(part, part, getattr(r, "mq_" + name).at[p, which]).wait()

    def ar_total(name, p):
        ar_wait(name, p, 1)
        return jnp.sum(getattr(r, f"ml{p}_{name}")[...], axis=0)

    def ar_start(name, rows):
        ar_send(name, 0, jnp.concatenate(rows, axis=0))

    def ar_mid(name):
        for p in range(last):
            ar_send(name, p + 1, ar_total(name, p))

    def ar_end(name):
        total = ar_total(name, last)
        return [total[i : i + 1, :] for i in range(msgs[name][0])]

    def ar_drain(name):
        for p in range(last + 1):
            ar_wait(name, p, 0)

    def halo_source(i, side):
        src = getattr(r, HALO[i][0])
        if HALO[i][0] == "dz2":
            return src.at[2 * side : 2 * side + 2, d.r2 // 2 :, :]
        if HALO[i][0] == "dva":
            return src.at[side * d.n : (side + 1) * d.n]
        return src.at[side]

    def halo_target(i, side):
        dst = getattr(r, HALO[i][1])
        if HALO[i][1] == "dva":
            return dst.at[(2 + side) * d.n : (3 + side) * d.n]
        return dst.at[side]

    def halo_copy(i, side):
        return pltpu.make_async_remote_copy(
            halo_source(i, side), halo_target(i, 1 - side), r.hsend.at[i, side], r.hrecv.at[i, 1 - side],
            device_id=(clip, tm + (2 * side - 1)), device_id_type=MESH,
        )

    def halo_start(i):
        @pl.when(tm > 0)
        def _():
            halo_copy(i, 0).start()

        @pl.when(tm < d.nt - 1)
        def _():
            halo_copy(i, 1).start()

    def halo_wait(i):
        lower, upper = halo_target(i, 0), halo_target(i, 1)

        @pl.when(tm > 0)
        def _():
            pltpu.make_async_copy(lower, lower, r.hrecv.at[i, 0]).wait()

        @pl.when(tm < d.nt - 1)
        def _():
            pltpu.make_async_copy(upper, upper, r.hrecv.at[i, 1]).wait()

        @pl.when(tm == 0)
        def _():
            lower[...] = jnp.zeros(lower.shape, lower.dtype)

        @pl.when(tm == d.nt - 1)
        def _():
            upper[...] = jnp.zeros(upper.shape, upper.dtype)

    def halo_drain(i):
        @pl.when(tm > 0)
        def _():
            pltpu.make_async_copy(
                halo_source(i, 0), halo_source(i, 0), r.hsend.at[i, 0]
            ).wait()

        @pl.when(tm < d.nt - 1)
        def _():
            pltpu.make_async_copy(
                halo_source(i, 1), halo_source(i, 1), r.hsend.at[i, 1]
            ).wait()

    order = {name: i for i, name in enumerate(NORMS)}
    width = dict(na=d.ca, da=d.ca, wa=d.c0, nb=d.cb, db=d.cb, wb=d.co, sb=d.co)

    def norm_set(name, sums, scale):
        i, c = order[name], width[name]
        inv = r.inv[:, :c] * scale
        mu = sums[0] * inv
        rs = lax.rsqrt(sums[1] * inv - mu * mu + epsilon)
        s = r.vec[2 * i : 2 * i + 1, :c] * rs
        r.par[i, 0:1, :c] = s
        r.par[i, 1:2, :c] = r.vec[2 * i + 1 : 2 * i + 2, :c] - mu * s
        r.par[i, 2:3, :c] = rs
        r.par[i, 3:4, :c] = mu

    def norm_of(name, lo, hi):
        i = order[name]
        return r.par[i, 0:1, lo:hi], r.par[i, 1:2, lo:hi]

    def back_set(name, sum_one, sum_two, scale):
        i, c = order[name], width[name]
        inv = r.inv[:, :c] * scale
        s, rs, mu = r.par[i, 0:1, :c], r.par[i, 2:3, :c], r.par[i, 3:4, :c]
        dgain = rs * (sum_two - mu * sum_one)
        gamma = s * rs * dgain * inv
        r.par[i, 4:5, :c] = s * sum_one * inv - gamma * mu
        r.par[i, 5:6, :c] = gamma
        r.small[2 * i : 2 * i + 1, :c] = dgain
        r.small[2 * i + 1 : 2 * i + 2, :c] = sum_one

    def back_of(name, lo, hi):
        i = order[name]
        return r.par[i, 0:1, lo:hi], r.par[i, 4:5, lo:hi], r.par[i, 5:6, lo:hi]

    def acc_clear(k, c):
        for i in range(k):
            r.acc[i, :, :c] = jnp.zeros((8, c), F32)

    def acc_rows(k, c):
        return [jnp.sum(r.acc[i, :, :c], axis=0, keepdims=True) for i in range(k)]

    def lanes(c, step=LANES):
        return [(lo, lo + step) for lo in range(0, c, step)]

    def slot_of(f):
        n = f // d.t
        return n * d.slots + 1 + (f - n * d.t)

    acc_clear(2, d.ca)
    weight_copy(0).wait()

    @pl.loop(0, d.f)
    def _(f):
        slot = lax.rem(f, 2)
        frame_copy(f, slot).wait()
        r.x[f] = jnp.zeros((d.h, d.wp, d.c0), BF16)
        r.x[f, :, 0 : d.w, :] = r.raw[slot]

        @pl.when(f + 2 < d.f)
        def _():
            frame_copy(f + 2, slot).start()

        v = dot(r.x[f].reshape(d.fr, d.c0), r.w_na[...])
        r.a1[f] = v
        m = mask_f(f)
        r.acc[0, :, : d.ca] += rows8(v) * m
        r.acc[1, :, : d.ca] += rows8(v * v) * m

    for n in range(d.n):
        r.dva[n] = r.a1[n * d.t].astype(BF16)
        r.dva[d.n + n] = r.a1[n * d.t + frames - 1].astype(BF16)
    pl.semaphore_wait(barrier, sum(size - 1 for _, _, size in d.phases))
    cells = (jnp.minimum(live, d.n) * frames * (d.h * d.w)).astype(F32)
    ar_start("na", acc_rows(2, d.ca) + [jnp.full((1, d.ca), 1.0, F32) * cells])
    halo_start(0)
    for i in range(3):
        src, dst = ((r.i_kta, r.kta), (r.i_ktb, r.ktb), (r.i_vec, r.vec))[i]
        pltpu.make_async_copy(src, dst, r.wsem.at[8 + i]).wait()
    for ref in (r.v1, r.v2):
        @pl.loop(0, d.n * d.slots)
        def _(i):
            zero = jnp.zeros((d.wp, ref.shape[2]), ref.dtype)
            ref[i, 0 : d.wp, :] = zero
            ref[i, d.er - d.wp : d.er, :] = zero
    weight_copy(1).wait()
    ar_mid("na")
    sums = ar_end("na")
    inv_cells = 1.0 / sums[2]
    for lo, hi in lanes(d.co, d.ca):
        r.inv[:, lo:hi] = inv_cells
    norm_set("na", sums, 1.0)

    half = float((d.h * d.w * 2) // (d.h2 * d.w2))

    def activated(v, name, lo, hi, cols, m):
        s, b = norm_of(name, lo, hi)
        return silu(v * s + b) * (cols * m)

    def mixed(hidden, weight):
        return dot(hidden, weight).astype(BF16)

    def inner(ref_in, hid, framed, name, weight, c, half_i):
        cols = full_cols

        @pl.loop(0, d.f)
        def _(f):
            m = mask_f(f)
            for lo, hi in lanes(c):
                hid[f, :, lo:hi] = activated(ref_in[f, :, lo:hi], name, lo, hi, cols, m).astype(BF16)
            framed[slot_of(f), d.wp : d.wp + d.fr, :] = mixed(hid[f], weight[...]).astype(framed.dtype)

        halo_wait(half_i)
        sides = (halo_target(half_i, 0), halo_target(half_i, 1))
        for n in range(d.n):
            for side in range(2):
                m = (has_prev, has_next)[side] * one(n < live)
                h = jnp.concatenate(
                    [
                        activated(sides[side][n, :, lo:hi].astype(F32), name, lo, hi, cols, m).astype(BF16)
                        for lo, hi in lanes(c)
                    ],
                    axis=1,
                )
                v = mixed(h, weight[...])
                if side == 0:
                    framed[n * d.slots, d.wp : d.wp + d.fr, :] = v.astype(framed.dtype)
                else:
                    for k in range(1, d.t):
                        at = (n * d.slots + 1 + k, slice(d.wp, d.wp + d.fr), slice(None))
                        framed[at] = (framed[at].astype(F32) + v.astype(F32) * one(frames == k)).astype(
                            framed.dtype
                        )
                    framed[n * d.slots + 1 + d.t, d.wp : d.wp + d.fr, :] = v.astype(framed.dtype)

    inner(r.a1, r.h1, r.v1, "na", r.w_ma, d.ca, 0)

    def taps(ref, lo):
        return [ref[i : i + 1, lo : lo + LANES] for i in range(27)]

    acc_clear(2, d.ca)

    @pl.loop(0, d.f)
    def _(f):
        base = slot_of(f) - 1
        m = mask_f(f)
        for lo, hi in lanes(d.ca):
            k = taps(r.kta, lo)
            one_sum = jnp.zeros((8, LANES), F32)
            two_sum = jnp.zeros((8, LANES), F32)
            for h in range(d.h):
                parts = [None] * 3
                for a in range(3):
                    for b in range(3):
                        v = r.v1[base + a, (h + b) * d.wp : (h + b + 1) * d.wp, lo:hi].astype(F32)
                        for e in range(3):
                            p = v * k[9 * a + 3 * b + e]
                            parts[e] = p if parts[e] is None else parts[e] + p
                o = parts[1] + pltpu.roll(parts[0], 1, 0) + pltpu.roll(parts[2], d.wp - 1, 0)
                o = o * row_cols
                r.d1[f, h * d.wp : (h + 1) * d.wp, lo:hi] = o
                one_sum += rows8(o)
                two_sum += rows8(o * o)
            r.acc[0, :, lo:hi] += one_sum * m
            r.acc[1, :, lo:hi] += two_sum * m

    ar_start("da", acc_rows(2, d.ca))
    weight_copy(2).wait()
    ar_mid("da")
    norm_set("da", ar_end("da"), 1.0)

    acc_clear(2, d.c0)

    @pl.loop(0, d.f)
    def _(f):
        m = mask_f(f)
        for lo, hi in lanes(d.ca):
            r.h2[f, :, lo:hi] = activated(r.d1[f, :, lo:hi], "da", lo, hi, full_cols, m).astype(BF16)
        for lo, hi in lanes(d.c0, 256):
            v = dot(r.h2[f], r.w_wa[:, lo:hi])
            r.a3[f, :, lo:hi] = v.astype(BF16)
            r.acc[0, :, lo:hi] += rows8(v)
            r.acc[1, :, lo:hi] += rows8(v * v)

    ar_start("wa", acc_rows(2, d.c0))
    weight_copy(3).wait()
    ar_mid("wa")
    norm_set("wa", ar_end("wa"), 1.0)

    def joined(f, lo, hi):
        s, b = norm_of("wa", lo, hi)
        x = r.x[f, :, :, lo:hi].reshape(d.fr, hi - lo).astype(F32)
        return r.a3[f, :, lo:hi].astype(F32) * s + b + x

    acc_clear(2, d.cb)

    @pl.loop(0, d.f)
    def _(f):
        m = mask_f(f)
        for lo, hi in lanes(d.c0):
            r.y1[f, :, lo:hi] = (silu(joined(f, lo, hi)) * (full_cols * m)).astype(BF16)
        for lo, hi in lanes(d.cb, 256):
            v = dot(r.y1[f], r.w_nb[:, lo:hi])
            r.b1[f, :, lo:hi] = v
            r.acc[0, :, lo:hi] += rows8(v)
            r.acc[1, :, lo:hi] += rows8(v * v)

    for n in range(d.n):
        r.hs2[0, n] = r.b1[n * d.t].astype(BF16)
        r.hs2[1, n] = r.b1[n * d.t + frames - 1].astype(BF16)
    ar_start("nb", acc_rows(2, d.cb))
    halo_start(1)

    rows_e = lax.broadcasted_iota(jnp.int32, (d.hr, d.fr), 0)
    cols_e = lax.broadcasted_iota(jnp.int32, (d.hr, d.fr), 1)
    pick = one(
        (cols_e == (rows_e // d.wh) * (2 * d.wp) + lax.rem(rows_e, d.wh) * 2)
    ).astype(BF16)

    @pl.loop(0, d.f2)
    def _(i):
        n = i // d.t2
        f = n * d.t + parity + 2 * (i - n * d.t2)
        for lo, hi in lanes(d.c0, 512):
            r.e[i, :, lo:hi] = dot(pick, r.y1[f, :, lo:hi])

    r.eb[...] = r.e[...].reshape(d.r2, d.c0).astype(BF16)
    weight_copy(6).wait()
    acc_clear(2, d.co)

    @pl.loop(0, d.co // d.cb)
    def _(j):
        for half_lo in range(0, d.cb, 256):
            at = pl.ds(pl.multiple_of(j * d.cb + half_lo, 256), 256)
            v = dot(r.eb[...], r.w_sb[:, at])
            r.b3s[d.co // d.cb + j, :, half_lo : half_lo + 256] = v
            r.acc[0, :, at] += rows8(v)
            r.acc[1, :, at] += rows8(v * v)

    ar_start("sk", acc_rows(2, d.co))
    weight_copy(4).wait()
    ar_mid("nb")
    norm_set("nb", ar_end("nb"), 1.0)

    inner(r.b1, r.g1, r.v2, "nb", r.w_mb, d.cb, 1)

    @pl.loop(0, d.f2)
    def _(i):
        n = i // d.t2
        base = n * d.slots + parity + 2 * (i - n * d.t2)
        for lo, hi in lanes(d.cb):
            k = taps(r.ktb, lo)
            for h in range(d.h2):
                parts = [None] * 3
                for a in range(3):
                    for b in range(3):
                        at = (2 * h + b) * d.wp
                        v = r.v2[base + a, at : at + d.wp, lo:hi].astype(F32)
                        for e in range(3):
                            p = v * k[9 * a + 3 * b + e]
                            parts[e] = p if parts[e] is None else parts[e] + p
                o = parts[1] + pltpu.roll(parts[0], 1, 0) + pltpu.roll(parts[2], d.wp - 1, 0)
                r.dz2[i, h * d.wp : (h + 1) * d.wp, lo:hi] = o

    hw = d.h2 * d.wp
    thin = one(
        lax.broadcasted_iota(jnp.int32, (d.hr, hw), 1)
        == 2 * lax.broadcasted_iota(jnp.int32, (d.hr, hw), 0)
    ).astype(BF16)

    def split(v):
        high = v.astype(BF16)
        rest = v - high.astype(F32)
        mid = rest.astype(BF16)
        return high, mid, (rest - mid.astype(F32)).astype(BF16)

    acc_clear(2, d.cb)

    @pl.loop(0, d.f2)
    def _(i):
        m = mask_o(i)
        for lo, hi in lanes(d.cb):
            v = sum(dot(thin, p) for p in split(r.dz2[i, :hw, lo:hi])) * half_cols
            r.d2[i, :, lo:hi] = v
            r.acc[0, :, lo:hi] += rows8(v) * m
            r.acc[1, :, lo:hi] += rows8(v * v) * m

    ar_start("db", acc_rows(2, d.cb))
    ar_mid("sk")
    weight_copy(5).wait()
    ar_mid("db")
    norm_set("sb", ar_end("sk"), half)
    norm_set("db", ar_end("db"), half)

    def d2_rows(ref, i, lo, hi):
        return ref[i, :, lo:hi]

    for i in range(d.f2):
        m = mask_o(i)
        for lo, hi in lanes(d.cb):
            g = activated(d2_rows(r.d2, i, lo, hi), "db", lo, hi, half_cols, m)
            r.e[i, :, lo:hi] = g
    r.g2[...] = r.e[:, :, : d.cb].reshape(d.r2, d.cb).astype(BF16)
    acc_clear(2, d.co)

    @pl.loop(0, d.co // d.cb)
    def _(j):
        for half_lo in range(0, d.cb, 256):
            at = pl.ds(pl.multiple_of(j * d.cb + half_lo, 256), 256)
            v = dot(r.g2[...], r.w_wb[:, at])
            r.b3s[j, :, half_lo : half_lo + 256] = v
            r.acc[0, :, at] += rows8(v)
            r.acc[1, :, at] += rows8(v * v)

    ar_start("wb", acc_rows(2, d.co))
    pltpu.make_async_copy(r.cotangent, r.cot, r.wsem.at[11]).wait()
    half_all = jnp.concatenate(
        [half_cols * mask_o(jnp.int32(i)) for i in range(d.f2)], axis=0
    )
    ar_mid("wb")
    norm_set("wb", ar_end("wb"), half)

    acc_clear(3, d.co)

    @pl.loop(0, d.co // LANES)
    def _(q):
        per = d.cb // LANES
        j = q // per
        at = pl.ds(pl.multiple_of((q - j * per) * LANES, LANES), LANES)
        lane = pl.ds(pl.multiple_of(q * LANES, LANES), LANES)
        i3, isk = order["wb"], order["sb"]
        b3, s = r.b3s[j, :, at], r.b3s[d.co // d.cb + j, :, at]
        z = b3 * r.par[i3, 0:1, lane] + r.par[i3, 1:2, lane]
        z = z + s * r.par[isk, 0:1, lane] + r.par[isk, 1:2, lane]
        g = logistic(z)
        y = (z * g * half_all).reshape(d.n, d.t2, d.h2, d.wh, LANES)
        sl = g * (1.0 + z * (1.0 - g)) * half_all
        for i in range(d.f2):
            n, t = i // d.t2, i % d.t2
            for h in range(d.h2):
                lo = i * d.hr + h * d.wh
                c = r.cot[n, t, h, :, lane].astype(F32)
                c = jnp.concatenate([c, jnp.zeros((d.wh - d.w2, LANES), F32)], axis=0)
                r.dz2[j, lo : lo + d.wh, at] = c * sl[lo : lo + d.wh, :]
        r.cot[:, :, :, :, lane] = y[:, :, :, : d.w2, :].astype(BF16)
        dz = r.dz2[j, :, at]
        r.acc[0, :, lane] += rows8(dz)
        r.acc[1, :, lane] += rows8(dz * b3)
        r.acc[2, :, lane] += rows8(dz * s)

    out_copy = pltpu.make_async_copy(r.cot, r.block_out, r.osem.at[0])
    out_copy.start()
    ar_start("gz", acc_rows(3, d.co))
    ar_mid("gz")
    sums = ar_end("gz")
    back_set("wb", sums[0], sums[1], half)
    back_set("sb", sums[0], sums[2], half)

    for lo in range(0, d.co, LANES):
        j, at = lo // d.cb, lo % d.cb
        dz = r.dz2[j, :, at : at + LANES]
        for name, off, dst in (("wb", 0, r.db3), ("sb", d.co // d.cb, r.ds)):
            al, be, ga = back_of(name, lo, lo + LANES)
            v = (dz * al - be - r.b3s[off + j, :, at : at + LANES] * ga) * half_all
            dst[:, lo : lo + LANES] = v.astype(BF16)

    acc_clear(2, d.cb)
    for lo, hi in lanes(d.cb, 256):
        g = dot_bt(r.db3[...], r.w_wb[lo:hi, :])
        for i in range(d.f2):
            s, b = norm_of("db", lo, hi)
            v = r.d2[i, :, lo:hi]
            dn = g[i * d.hr : (i + 1) * d.hr, :] * slope(v * s + b)
            r.dz2[i, : d.hr, lo:hi] = dn
            r.acc[0, :, lo:hi] += rows8(dn)
            r.acc[1, :, lo:hi] += rows8(dn * v)
    for n in range(d.n):
        for side, j in ((0, 0), (1, out_frames - 1)):
            at = d.r2 // 2 + n * d.hr
            r.dz2[2 * side, at : at + d.hr, :] = r.dz2[n * d.t2 + j, : d.hr, :]
            r.dz2[2 * side + 1, at : at + d.hr, :] = r.d2[n * d.t2 + j]
    ar_start("gdb", acc_rows(2, d.cb))
    halo_start(2)

    def weight_grad(name, x, y, step):
        w = getattr(r, "w_" + name)
        for lo in range(0, w.shape[1], step):
            w[:, lo : lo + step] = dot_at(x, y(lo, lo + step)).astype(BF16)
        i = WEIGHTS.index(name)
        pltpu.make_async_copy(w, getattr(r, "o_" + name), r.osem.at[1 + i]).start()

    for lo, hi in lanes(d.c0, 256):
        v = dot_bt(r.ds[...], r.w_sb[lo:hi, :])
        for i in range(d.f2):
            r.e[i, :, lo:hi] = v[i * d.hr : (i + 1) * d.hr, :]
    weight_grad("wb", r.g2[...], lambda lo, hi: r.db3[:, lo:hi], 512)
    ar_mid("gdb")
    weight_grad("sb", r.eb[...], lambda lo, hi: r.ds[:, lo:hi], 256)
    back_set("db", *ar_end("gdb"), half)

    per = d.ca // LANES
    spread = one(
        lax.broadcasted_iota(jnp.int32, (hw, d.hr), 0)
        == 2 * lax.broadcasted_iota(jnp.int32, (hw, d.hr), 1)
    ).astype(BF16)

    def u_at(slot, row, rows, lo):
        at = (lo // d.ca) * d.ur
        return (slot, slice(at + row, at + row + rows), slice(lo % d.ca, lo % d.ca + LANES))

    @pl.loop(0, d.n * d.slots)
    def _(i):
        r.u[i] = jnp.zeros((d.er, d.ca), F32)

    def grad_d2(dn, v, lo, m):
        al, be, ga = back_of("db", lo, lo + LANES)
        g = (dn * al - be - v * ga) * (half_cols * m)
        return sum(dot(spread, p) for p in split(g))

    halo_wait(2)
    for n in range(d.n):
        for lo in range(0, d.cb, LANES):
            own = [
                grad_d2(r.dz2[n * d.t2 + j, : d.hr, lo : lo + LANES], r.d2[n * d.t2 + j, :, lo : lo + LANES],
                        lo, mask_o(jnp.int32(n * d.t2 + j)))
                for j in range(d.t2)
            ]
            before = grad_d2(
                r.hr3[0, 0, n * d.hr : (n + 1) * d.hr, lo : lo + LANES], r.hr3[0, 1, n * d.hr : (n + 1) * d.hr, lo : lo + LANES], lo,
                has_prev * one(n < live) * one(parity == 1),
            )
            after = grad_d2(
                r.hr3[1, 0, n * d.hr : (n + 1) * d.hr, lo : lo + LANES], r.hr3[1, 1, n * d.hr : (n + 1) * d.hr, lo : lo + LANES], lo,
                has_next * one(n < live) * one(((start + frames) & 1) == 0),
            )
            base = n * d.slots
            r.u[u_at(base, 0, hw, lo)] = before
            for i in range(1, d.t + 2):
                v = jnp.zeros((hw, LANES), F32)
                for j in range(d.t2):
                    p = i - 1 - 2 * j
                    if p in (0, 1):
                        v = v + own[j] * one(parity == p)
                if i >= 3:
                    v = v + after * one(frames + 1 == i)
                r.u[u_at(base + i, 0, hw, lo)] = v

    acc_clear(2, d.cb)

    @pl.loop(0, d.f)
    def _(f):
        base = slot_of(f)
        m = mask_f(f)
        for lo, hi in lanes(d.cb):
            k = taps(r.ktb, lo)
            for h in range(d.h):
                rows = ((h // 2, 1),) if h % 2 == 0 else ((h // 2 + 1, 0), (h // 2, 2))
                parts = [None] * 3
                for a in range(3):
                    for row, b in rows:
                        if row >= d.h2:
                            continue
                        v = r.u[u_at(base + 1 - a, row * d.wp, d.wp, lo)]
                        for e in range(3):
                            p = v * k[9 * a + 3 * b + e]
                            parts[e] = p if parts[e] is None else parts[e] + p
                o = parts[1] + pltpu.roll(parts[0], d.wp - 1, 0) + pltpu.roll(parts[2], 1, 0)
                r.dvb[f, h * d.wp : (h + 1) * d.wp, lo:hi] = o.astype(BF16)
        for lo, hi in lanes(d.cb, 256):
            g = dot_bt(r.dvb[f], r.w_mb[lo:hi, :])
            for at in range(lo, hi, LANES):
                s, b = norm_of("nb", at, at + LANES)
                v = r.b1[f, :, at : at + LANES]
                dn = g[:, at - lo : at - lo + LANES] * slope(v * s + b) * (full_cols * m)
                r.b3s[f, :, at : at + LANES] = dn
                r.acc[0, :, at : at + LANES] += rows8(dn)
                r.acc[1, :, at : at + LANES] += rows8(dn * v)

    ar_start("gnb", acc_rows(2, d.cb))

    def shifted(v):
        return (pltpu.roll(v, d.wp - 1, 0), v, pltpu.roll(v, 1, 0))

    for lo in range(0, d.cb, LANES):
        def body(i, sums):
            n = i // d.t2
            slot = n * d.slots + parity + 2 * (i - n * d.t2)
            sums = list(sums)
            for h in range(d.h2):
                g = shifted(r.u[u_at(slot + 1, h * d.wp, d.wp, lo)] * mask_o(i))
                for a in range(3):
                    for b in range(3):
                        at = (2 * h + b) * d.wp
                        v = r.v2[slot + a, at : at + d.wp, lo : lo + LANES].astype(F32)
                        for e in range(3):
                            sums[9 * a + 3 * b + e] += rows8(v * g[e])
            return tuple(sums)

        sums = lax.fori_loop(0, d.f2, body, (jnp.zeros((8, LANES), F32),) * 27)
        for i in range(27):
            r.gkb[i : i + 1, lo : lo + LANES] = jnp.sum(sums[i], axis=0, keepdims=True)

    def flat(ref):
        return ref[...].reshape(d.f * d.fr, ref.shape[-1])

    ar_mid("gnb")
    weight_grad("mb", flat(r.g1), lambda lo, hi: r.dvb[:, :, lo:hi].reshape(d.f * d.fr, hi - lo), 256)
    back_set("nb", *ar_end("gnb"), 1.0)

    acc_clear(2, d.c0)

    @pl.loop(0, d.f)
    def _(f):
        m = mask_f(f)
        n = f // d.t
        t = f - n * d.t
        for lo, hi in lanes(d.cb):
            al, be, ga = back_of("nb", lo, hi)
            v = (r.b3s[f, :, lo:hi] * al - be - r.b1[f, :, lo:hi] * ga) * (full_cols * m)
            r.dvb[f, :, lo:hi] = v.astype(BF16)
        j = jnp.clip((t - parity) // 2, 0, d.t2 - 1)
        flag = one(((t - parity) & 1) == 0)
        for lo, hi in lanes(d.c0, 256):
            g = dot_bt(r.dvb[f], r.w_nb[lo:hi, :])
            for at in range(lo, hi, LANES):
                parts = split(r.e[n * d.t2 + j, :, at : at + LANES] * flag)
                up = sum(dot_at(pick, p) for p in parts[:2])
                z = joined(f, at, at + LANES)
                dz = (g[:, at - lo : at - lo + LANES] + up) * slope(z) * (full_cols * m)
                r.dz1[f, :, at : at + LANES] = dz.astype(BF16)
                v = r.a3[f, :, at : at + LANES].astype(F32)
                r.acc[0, :, at : at + LANES] += rows8(dz)
                r.acc[1, :, at : at + LANES] += rows8(dz * v)

    ar_start("gwa", acc_rows(2, d.c0))
    ar_mid("gwa")
    weight_grad("nb", flat(r.y1), lambda lo, hi: r.dvb[:, :, lo:hi].reshape(d.f * d.fr, hi - lo), 256)
    back_set("wa", *ar_end("gwa"), 1.0)

    acc_clear(2, d.ca)

    @pl.loop(0, d.f)
    def _(f):
        m = mask_f(f)
        for lo, hi in lanes(d.c0):
            al, be, ga = back_of("wa", lo, hi)
            v = r.dz1[f, :, lo:hi].astype(F32) * al - be - r.a3[f, :, lo:hi].astype(F32) * ga
            r.a3[f, :, lo:hi] = (v * (full_cols * m)).astype(BF16)
        g = dot_bt(r.a3[f], r.w_wa[...])
        for lo, hi in lanes(d.ca):
            s, b = norm_of("da", lo, hi)
            v = r.d1[f, :, lo:hi]
            dn = g[:, lo:hi] * slope(v * s + b)
            r.u[slot_of(f), d.wp : d.wp + d.fr, lo:hi] = dn
            r.acc[0, :, lo:hi] += rows8(dn)
            r.acc[1, :, lo:hi] += rows8(dn * v)

    halo_drain(1)
    for n in range(d.n):
        for side, k in ((0, 0), (1, frames - 1)):
            r.hs2[side, n, :, : d.ca] = r.u[n * d.slots + 1 + k, d.wp : d.wp + d.fr, :].astype(BF16)
            r.hs2[side, n, :, d.ca :] = r.d1[n * d.t + k].astype(BF16)
    ar_start("gda", acc_rows(2, d.ca))
    halo_start(3)
    ar_mid("gda")
    weight_grad("wa", flat(r.h2), lambda lo, hi: r.a3[:, :, lo:hi].reshape(d.f * d.fr, hi - lo), 256)

    @pl.loop(0, d.n * d.slots)
    def _(i):
        zero = jnp.zeros((d.wp, d.ca), F32)
        r.u[i, 0 : d.wp, :] = zero
        r.u[i, d.er - d.wp : d.er, :] = zero

    back_set("da", *ar_end("gda"), 1.0)

    def grad_d1(dn, v, lo, hi, m):
        al, be, ga = back_of("da", lo, hi)
        return (dn * al - be - v * ga) * (full_cols * m)

    mid_rows = slice(d.wp, d.wp + d.fr)

    @pl.loop(0, d.f)
    def _(f):
        m = mask_f(f)
        for lo, hi in lanes(d.ca):
            r.u[slot_of(f), mid_rows, lo:hi] = grad_d1(
                r.u[slot_of(f), mid_rows, lo:hi], r.d1[f, :, lo:hi], lo, hi, m
            )

    halo_wait(3)
    for n in range(d.n):
        for lo, hi in lanes(d.ca):
            r.u[n * d.slots, mid_rows, lo:hi] = grad_d1(
                r.hr2[0, n, :, lo:hi].astype(F32), r.hr2[0, n, :, d.ca + lo : d.ca + hi].astype(F32), lo, hi,
                has_prev * one(n < live),
            )
            v = grad_d1(
                r.hr2[1, n, :, lo:hi].astype(F32), r.hr2[1, n, :, d.ca + lo : d.ca + hi].astype(F32), lo, hi,
                has_next * one(n < live),
            )
            for k in range(1, d.t):
                at = n * d.slots + 1 + k
                r.u[at, mid_rows, lo:hi] = r.u[at, mid_rows, lo:hi] + v * one(frames == k)
            r.u[n * d.slots + 1 + d.t, mid_rows, lo:hi] = v

    halo_drain(0)
    acc_clear(2, d.ca)

    @pl.loop(0, d.f)
    def _(f):
        base = slot_of(f)
        m = mask_f(f)
        for lo, hi in lanes(d.ca):
            k = taps(r.kta, lo)
            for h in range(d.h):
                parts = [None] * 3
                for a in range(3):
                    for b in range(3):
                        v = r.u[base + 1 - a, (h + 2 - b) * d.wp : (h + 3 - b) * d.wp, lo:hi]
                        for e in range(3):
                            p = v * k[9 * a + 3 * b + e]
                            parts[e] = p if parts[e] is None else parts[e] + p
                o = parts[1] + pltpu.roll(parts[0], d.wp - 1, 0) + pltpu.roll(parts[2], 1, 0)
                r.dva[f, h * d.wp : (h + 1) * d.wp, lo:hi] = o.astype(BF16)
        g = dot_bt(r.dva[f], r.w_ma[...])
        for lo, hi in lanes(d.ca):
            s, b = norm_of("na", lo, hi)
            v = r.a1[f, :, lo:hi]
            dn = g[:, lo:hi] * slope(v * s + b) * (full_cols * m)
            r.d1[f, :, lo:hi] = dn
            r.acc[0, :, lo:hi] += rows8(dn)
            r.acc[1, :, lo:hi] += rows8(dn * v)

    ar_start("gna", acc_rows(2, d.ca))

    for lo in range(0, d.ca, LANES):
        def body(f, sums):
            slot = slot_of(f)
            m = mask_f(f)
            sums = list(sums)
            for h in range(d.h):
                g = shifted(r.u[slot, (h + 1) * d.wp : (h + 2) * d.wp, lo : lo + LANES] * m)
                for a in range(3):
                    for b in range(3):
                        at = (h + b) * d.wp
                        v = r.v1[slot - 1 + a, at : at + d.wp, lo : lo + LANES].astype(F32)
                        for e in range(3):
                            sums[9 * a + 3 * b + e] += rows8(v * g[e])
            return tuple(sums)

        sums = lax.fori_loop(0, d.f, body, (jnp.zeros((8, LANES), F32),) * 27)
        for i in range(27):
            r.gka[i : i + 1, lo : lo + LANES] = jnp.sum(sums[i], axis=0, keepdims=True)

    ar_mid("gna")
    weight_grad("ma", flat(r.h1), lambda lo, hi: r.dva[:, :, lo:hi].reshape(d.f * d.fr, hi - lo), 256)
    back_set("na", *ar_end("gna"), 1.0)

    def grad_copy(f, slot):
        return pltpu.make_async_copy(
            r.raw.at[slot], r.input_grad.at[f // d.t, f % d.t], r.isem.at[slot]
        )

    @pl.loop(0, d.f)
    def _(f):
        m = mask_f(f)
        slot = lax.rem(f, 2)
        for lo, hi in lanes(d.ca):
            al, be, ga = back_of("na", lo, hi)
            v = (r.d1[f, :, lo:hi] * al - be - r.a1[f, :, lo:hi] * ga) * (full_cols * m)
            r.dva[f, :, lo:hi] = v.astype(BF16)

        @pl.when(f >= 2)
        def _():
            grad_copy(f - 2, slot).wait()

        for lo, hi in lanes(d.c0, 256):
            g = dot_bt(r.dva[f], r.w_na[lo:hi, :]) + r.dz1[f, :, lo:hi].astype(F32)
            g = g.astype(BF16).reshape(d.h, d.wp, hi - lo)
            r.raw[slot, :, :, lo:hi] = g[:, : d.w, :]
        grad_copy(f, slot).start()

    weight_grad("na", flat2(r.x, d), lambda lo, hi: r.dva[:, :, lo:hi].reshape(d.f * d.fr, hi - lo), 256)
    for i, (src, dst) in enumerate(((r.small, r.o_small), (r.gka, r.o_gka), (r.gkb, r.o_gkb))):
        pltpu.make_async_copy(src, dst, r.osem.at[8 + i]).start()

    grad_copy(d.f - 2, d.f % 2).wait()
    grad_copy(d.f - 1, (d.f - 1) % 2).wait()
    out_copy.wait()
    for i, name in enumerate(WEIGHTS):
        pltpu.make_async_copy(getattr(r, "w_" + name), getattr(r, "o_" + name), r.osem.at[1 + i]).wait()
    for i, (src, dst) in enumerate(((r.small, r.o_small), (r.gka, r.o_gka), (r.gkb, r.o_gkb))):
        pltpu.make_async_copy(src, dst, r.osem.at[8 + i]).wait()
    for name in msgs:
        ar_drain(name)
    for i in (2, 3):
        halo_drain(i)


def flat2(ref, d):
    return ref[...].reshape(d.f * d.fr, d.c0)


def per_device(mesh, *args):
    (
        clip_in, cotangent, frame_count, clip_count, narrow_a, narrow_gain_a, narrow_bias_a, mixing_a,
        depthwise_a, depth_gain_a, depth_bias_a, widen_a, widen_gain_a, widen_bias_a, narrow_b,
        narrow_gain_b, narrow_bias_b, mixing_b, depthwise_b, depth_gain_b, depth_bias_b, widen_b,
        widen_gain_b, widen_bias_b, shortcut_b, shortcut_gain_b, shortcut_bias_b,
    ) = args
    d = Dims(mesh, clip_in.shape, cotangent.shape, narrow_a.shape[1], narrow_b.shape[1])
    vectors = (
        narrow_gain_a, narrow_bias_a, depth_gain_a, depth_bias_a, widen_gain_a, widen_bias_a,
        narrow_gain_b, narrow_bias_b, depth_gain_b, depth_bias_b, widen_gain_b, widen_bias_b,
        shortcut_gain_b, shortcut_bias_b,
    )
    packed = jnp.stack([jnp.pad(v, (0, d.co - v.shape[0])) for v in vectors] + [jnp.zeros((d.co,), F32)] * 2)

    def taps_of(k):
        return jnp.pad(k.astype(F32).T, ((0, 5), (0, 0)))

    scratch = scratch_of(d)
    names = INPUTS + OUTPUTS + tuple(scratch)
    shapes = dict(
        block_out=jax.ShapeDtypeStruct(cotangent.shape, BF16),
        input_grad=jax.ShapeDtypeStruct(clip_in.shape, BF16),
        o_small=jax.ShapeDtypeStruct((16, d.co), F32),
        o_gka=jax.ShapeDtypeStruct((32, d.ca), F32),
        o_gkb=jax.ShapeDtypeStruct((32, d.cb), F32),
        o_na=jax.ShapeDtypeStruct(narrow_a.shape, BF16),
        o_ma=jax.ShapeDtypeStruct(mixing_a.shape, BF16),
        o_wa=jax.ShapeDtypeStruct(widen_a.shape, BF16),
        o_nb=jax.ShapeDtypeStruct(narrow_b.shape, BF16),
        o_mb=jax.ShapeDtypeStruct(mixing_b.shape, BF16),
        o_wb=jax.ShapeDtypeStruct(widen_b.shape, BF16),
        o_sb=jax.ShapeDtypeStruct(shortcut_b.shape, BF16),
    )
    anywhere = pl.BlockSpec(memory_space=pl.ANY)
    scalars = pl.BlockSpec(memory_space=pltpu.SMEM)
    outs = pl.pallas_call(
        functools.partial(kernel, d, names),
        out_shape=[shapes[name] for name in OUTPUTS],
        in_specs=[scalars if name.endswith("_count") else anywhere for name in INPUTS],
        out_specs=[anywhere] * len(OUTPUTS),
        scratch_shapes=list(scratch.values()),
        compiler_params=pltpu.CompilerParams(
            collective_id=0, has_side_effects=True, vmem_limit_bytes=63 * 1024 * 1024
        ),
    )(
        clip_in, cotangent, frame_count, clip_count, narrow_a, mixing_a, widen_a, narrow_b, mixing_b,
        widen_b, shortcut_b, taps_of(depthwise_a), taps_of(depthwise_b), packed,
    )
    out = dict(zip(OUTPUTS, outs))

    def share(g):
        part = lax.psum_scatter(g.astype(BF16), "tm", scatter_dimension=0, tiled=True)
        return lax.psum(part, "clip").astype(F32)

    def share_taps(g):
        return share(g[:27].T)

    small = out["o_small"]
    grads = [small[i, : v.shape[0]] for i, v in enumerate(vectors)]
    return (
        out["block_out"], out["input_grad"],
        share(out["o_na"]), grads[0], grads[1], share(out["o_ma"]), share_taps(out["o_gka"]),
        grads[2], grads[3], share(out["o_wa"]), grads[4], grads[5],
        share(out["o_nb"]), grads[6], grads[7], share(out["o_mb"]), share_taps(out["o_gkb"]),
        grads[8], grads[9], share(out["o_wb"]), grads[10], grads[11],
        share(out["o_sb"]), grads[12], grads[13],
    )


def solution(mesh):
    data = P("clip", "tm", None, None, None)
    rows = P("tm", None)
    in_specs = (data, data, P(), P("clip")) + (P(),) * 23
    block = (rows, P(), P(), rows, rows, P(), P(), rows, P(), P())
    out_specs = (data, data) + block + block + (rows, P(), P())
    return jax.shard_map(
        functools.partial(per_device, mesh), mesh=mesh, in_specs=in_specs, out_specs=out_specs,
        check_vma=False,
    )
```

```python
import functools

import jax
import jax.numpy as jnp
from jax import lax
from jax.experimental import pallas as pl
from jax.experimental.pallas import tpu as pltpu
from jax.sharding import PartitionSpec as P

epsilon = 1e-05
LANES = 128
MESH = pl.DeviceIdType.MESH
F32 = jnp.float32
BF16 = jnp.bfloat16

NORMS = ("na", "da", "wa", "nb", "db", "wb", "sb")


HALO = (("dva", "dva"), ("hs2", "hr2"), ("dz2", "hr3"), ("hs2", "hr2"))


class Refs:
    pass


def logistic(z):
    return 0.5 * jnp.tanh(0.5 * z) + 0.5


def silu(z):
    return z * logistic(z)


def slope(z):
    q = logistic(z)
    return q * (1.0 + z * (1.0 - q))


def dot(x, w):
    return jnp.dot(x, w, preferred_element_type=F32)


def dot_bt(x, w):
    return lax.dot_general(x, w, (((1,), (1,)), ((), ())), preferred_element_type=F32)


def dot_at(x, y):
    return lax.dot_general(x, y, (((0,), (0,)), ((), ())), preferred_element_type=F32)


def rows8(v):
    return jnp.sum(v.reshape(v.shape[0] // 8, 8, v.shape[1]), axis=0)


def tile_lanes(v, width):
    if width == v.shape[1]:
        return v
    return jnp.concatenate([v] * (width // v.shape[1]), axis=1)


class Piece:
    def __init__(self, d, name, weight, rows, lo, hi, first, split):
        self.name, self.weight, self.lo, self.hi = name, weight, lo, hi
        self.n, self.rb = hi - lo, rows // d.nt
        self.first, self.split = first, split
        self.shape1 = self.cut((self.rb, self.n), split[0])
        self.shape2 = self.cut(self.shape1, split[1])

    @staticmethod
    def cut(shape, axis):
        return (shape[0] // 2, shape[1]) if axis == "r" else (shape[0], shape[1] // 2)

    def window(self, level, bit):
        rows, cols = self.shape1 if level == 1 else self.shape2
        if self.split[level - 1] == "r":
            at = bit * rows
            return (pl.ds(at if isinstance(at, int) else pl.multiple_of(at, rows), rows), slice(None))
        at = bit * cols
        return (slice(None), pl.ds(at if isinstance(at, int) else pl.multiple_of(at, cols), cols))


def pieces_of(d):
    half = d.co // 2
    return [
        Piece(d, "wb", "wb", d.cb, 0, d.co, "x", "rr"),
        Piece(d, "sb0", "sb", d.c0, 0, half, "y", "rr"),
        Piece(d, "sb1", "sb", d.c0, half, d.co, "x", "rr"),
        Piece(d, "nb", "nb", d.c0, 0, d.cb, "y", "rr"),
        Piece(d, "mb", "mb", d.cb, 0, d.cb, "x", "rr"),
        Piece(d, "wa", "wa", d.ca, 0, d.c0, "y", "cc"),
        Piece(d, "na", "na", d.c0, 0, d.ca, "x", "rr"),
        Piece(d, "ma", "ma", d.ca, 0, d.ca, "y", "cr"),
    ]


class Dims:
    def __init__(self, mesh, clip_in, cotangent, ca, cb):
        self.nc = mesh.shape["clip"]
        self.nt = mesh.shape["tm"]
        self.phases = [("tm", 1, self.nt)] if self.nt <= 8 else [("tm", 1, 8), ("tm", 8, self.nt // 8)]
        self.phases.append(("clip", 1, self.nc))
        self.n, self.t, self.h, self.w, self.c0 = clip_in
        self.ca, self.cb = ca, cb
        self.co = cotangent[-1]
        self.wp = -(-(self.w + 1) // 16) * 16
        self.f = self.n * self.t
        self.fr = self.h * self.wp
        self.er = (self.h + 2) * self.wp
        self.slots = self.t + 2
        self.t2, self.h2, self.w2 = self.t // 2, self.h // 2, self.w // 2
        self.wh = self.wp // 2
        self.f2 = self.n * self.t2
        self.hr = self.h2 * self.wh
        self.r2 = self.f2 * self.hr
        self.ur = (self.h2 + 1) * self.wp
        self.staged = self.nt == 8 and self.nc == 4
        self.nz = self.nt // 2
        self.pieces = pieces_of(self) if self.staged else []


def messages(d):
    return dict(
        na=(3, d.ca), da=(2, d.ca), wa=(2, d.c0), nb=(2, d.cb), sk=(2, d.co), db=(2, d.cb),
        wb=(2, d.co), gz=(3, d.co), gdb=(2, d.cb), gnb=(2, d.cb), gwa=(2, d.c0), gda=(2, d.ca),
        gna=(2, d.ca), ka=(32, d.ca), kb=(32, d.cb),
    )


def scratch_of(d):
    V = pltpu.VMEM
    DM = pltpu.SemaphoreType.DMA
    s = dict(
        x=V((d.f, d.fr, d.c0), BF16),
        a1=V((d.f, d.fr, d.ca), BF16),
        h1=V((d.f, d.fr, d.ca), BF16),
        v1=V((d.n * d.slots, d.er, d.ca), BF16),
        d1=V((d.f, d.fr, d.ca), F32),
        h2=V((d.f, d.fr, d.ca), BF16),
        a3=V((d.f, d.fr, d.c0), BF16),
        y1=V((d.f, d.fr, d.c0), BF16),
        b1=V((d.f, d.fr, d.cb), BF16),
        g1=V((d.f, d.fr, d.cb), BF16),
        v2=V((d.n * d.slots, d.er, d.cb), BF16),
        d2=V((d.f2, d.hr, d.cb), F32),
        g2=V((d.r2, d.cb), BF16),
        e=V((d.f2, d.hr, d.c0), F32),
        eb=V((d.r2, d.c0), BF16),
        b3s=V((2 * (d.co // d.cb), d.r2, d.cb), F32),
        dz2=V((d.co // d.cb, d.r2, d.cb), F32),
        db3=V((d.r2, d.co), BF16),
        ds=V((d.r2, d.co), BF16),
        u=V((d.n * d.slots, d.er, d.ca), F32),
        dvb=V((d.f, d.fr, d.cb), BF16),
        dva=V((max(d.f, 4 * d.n), d.fr, d.ca), BF16),
        acc=V((3, 8, d.co), F32),
        inv=V((1, d.co), F32),
        kta=V((32, d.ca), F32),
        ktb=V((32, d.cb), F32),
        vec=V((16, d.co), F32),
        gka=V((32, d.ca), F32),
        gkb=V((32, d.cb), F32),
        par=V((len(NORMS), 8, d.co), F32),
        hs2=V((2, d.n, d.fr, d.cb), BF16),
        hr2=V((2, d.n, d.fr, d.cb), BF16),
        hr3=V((2, 2, d.n * d.hr, d.cb), F32),
        hsend=DM((4, 2)),
        hrecv=DM((4, 2)),
        w_na=V((d.c0, d.ca), BF16),
        w_ma=V((d.ca, d.ca), BF16),
        w_wa=V((d.ca, d.c0), BF16),
        w_nb=V((d.c0, d.cb), BF16),
        w_mb=V((d.cb, d.cb), BF16),
        w_wb=V((d.cb, d.co), BF16),
        w_sb=V((d.c0, d.co), BF16),
        small=V((16, d.co), F32),
        wsem=DM((16,)),
        xsem=DM((d.f,)),
        osem=DM((24,)),
        gsem=DM((8, 4)),
        isem=DM((d.f,)),
    )
    for name, (k, c) in messages(d).items():
        kind = BF16 if k == 32 else F32
        for p, (_, _, size) in enumerate(d.phases):
            s[f"ms{p}_{name}"] = V((k, c), kind)
            s[f"ml{p}_{name}"] = V((size, k, c), kind)
        s["mq_" + name] = DM((len(d.phases), 2))
    for p in d.pieces:
        s["gs_" + p.name] = DM((5, 2))
        s["gc_" + p.name] = V((d.nz, p.rb, p.n), BF16)
        s["g1_" + p.name] = V((d.nz,) + p.shape1, BF16)
        s["g2_" + p.name] = V((d.nz,) + p.shape2, BF16)
        s["g3_" + p.name] = V((d.nz,) + p.shape2, BF16)
        s["g4_" + p.name] = V((d.nc,) + p.shape2, BF16)
    return s


INPUTS = (
    "clip_in", "cotangent", "frame_count", "clip_count", "i_na", "i_ma", "i_wa", "i_nb", "i_mb",
    "i_wb", "i_sb", "i_kta", "i_ktb", "i_vec",
)
OUTPUTS = (
    "block_out", "input_grad", "o_small", "o_gka", "o_gkb", "o_na", "o_ma", "o_wa", "o_nb", "o_mb",
    "o_wb", "o_sb",
)
WEIGHTS = ("na", "ma", "wa", "nb", "mb", "wb", "sb")


def kernel(d, names, *refs):
    r = Refs()
    for name, ref in zip(names, refs):
        setattr(r, name, ref)
    clip = lax.axis_index("clip")
    tm = lax.axis_index("tm")
    msgs = messages(d)

    def weight_copy(i):
        name = WEIGHTS[i]
        return pltpu.make_async_copy(
            getattr(r, "i_" + name), getattr(r, "w_" + name), r.wsem.at[i]
        )

    def frame_copy(f):
        return pltpu.make_async_copy(r.clip_in.at[f], r.x.at[f], r.xsem.at[f])

    frame_copy(0).start()
    weight_copy(0).start()
    for f in range(1, d.f):
        frame_copy(f).start()
    for i, (src, dst) in enumerate(
        ((r.i_kta, r.kta), (r.i_ktb, r.ktb), (r.i_vec, r.vec), (r.cotangent, r.ds))
    ):
        pltpu.make_async_copy(src, dst, r.wsem.at[8 + i]).start()
    for i in range(1, len(WEIGHTS)):
        weight_copy(i).start()

    barrier = pltpu.get_barrier_semaphore()

    def place(p):
        axis, stride, size = d.phases[p]
        return lax.rem((clip if axis == "clip" else tm) // stride, size)

    def peer(p, k):
        axis, stride, size = d.phases[p]
        shift = (lax.rem(place(p) + k, size) - place(p)) * stride
        return (clip + shift, tm) if axis == "clip" else (clip, tm + shift)

    for p in range(len(d.phases)):
        @pl.loop(1, d.phases[p][2])
        def _(k):
            pl.semaphore_signal(barrier, 1, device_id=peer(p, k), device_id_type=MESH)

    frames = jnp.clip(r.frame_count[tm], 2, d.t)
    start = lax.fori_loop(
        0, d.nt, lambda i, s: s + jnp.where(i < tm, r.frame_count[i], 0), jnp.int32(0)
    )
    parity = start & 1
    out_frames = jnp.clip((frames + 1 - parity) // 2, 1, d.t2)
    live = r.clip_count[0]

    def one(cond):
        return jnp.where(cond, 1.0, 0.0).astype(F32)

    def mask_f(f):
        return one((lax.rem(f, d.t) < frames) & (f // d.t < live))

    def mask_o(i):
        return one((lax.rem(i, d.t2) < out_frames) & (i // d.t2 < live))

    has_prev = one(tm > 0)
    has_next = one(tm < d.nt - 1)

    full_cols = one(lax.rem(lax.broadcasted_iota(jnp.int32, (d.fr, LANES), 0), d.wp) < d.w)
    half_cols = one(lax.rem(lax.broadcasted_iota(jnp.int32, (d.hr, LANES), 0), d.wh) < d.w2)
    row_cols = one(lax.broadcasted_iota(jnp.int32, (d.wp, LANES), 0) < d.w)

    last = len(d.phases) - 1

    def ar_send(name, p, value):
        src, slots = getattr(r, f"ms{p}_{name}"), getattr(r, f"ml{p}_{name}")
        q = getattr(r, "mq_" + name)
        src[...] = value.astype(src.dtype)

        @pl.loop(1, d.phases[p][2])
        def _(k):
            pltpu.make_async_remote_copy(
                src, slots.at[place(p)], q.at[p, 0], q.at[p, 1], device_id=peer(p, k),
                device_id_type=MESH,
            ).start()

        slots[place(p)] = value.astype(src.dtype)

    def ar_wait(name, p, which):
        part = getattr(r, f"ml{p}_{name}").at[pl.ds(0, d.phases[p][2] - 1)]
        pltpu.make_async_copy(part, part, getattr(r, "mq_" + name).at[p, which]).wait()

    def ar_total(name, p):
        ar_wait(name, p, 1)
        return jnp.sum(getattr(r, f"ml{p}_{name}")[...].astype(F32), axis=0)

    def ar_start(name, rows):
        ar_send(name, 0, jnp.concatenate(rows, axis=0))

    def ar_mid(name):
        for p in range(last):
            ar_send(name, p + 1, ar_total(name, p))

    def ar_end(name):
        total = ar_total(name, last)
        if msgs[name][0] == 32:
            return total
        return [total[i : i + 1, :] for i in range(msgs[name][0])]

    def ar_drain(name):
        for p in range(last + 1):
            ar_wait(name, p, 0)

    core, zed = lax.rem(tm, 2), tm // 2
    bit = dict(x=lax.rem(clip, 2), y=clip // 2)
    step = dict(x=1 - 2 * bit["x"], y=2 - 4 * bit["y"])

    def block(p, i):
        if p.weight in ("na", "nb"):
            per = d.er // p.rb
            ref = r.v1 if p.weight == "na" else r.v2
            return ref.at[i // per, pl.ds(pl.multiple_of(lax.rem(i, per) * p.rb, p.rb), p.rb), :]
        return getattr(r, "w_" + p.weight).at[pl.ds(pl.multiple_of(i * p.rb, p.rb), p.rb), p.lo : p.hi]

    def bits(p):
        return (bit["x"], bit["y"]) if p.first == "x" else (bit["y"], bit["x"])

    def stage_copy(p, stage, src, dst, clip_at, tm_at):
        q = getattr(r, "gs_" + p.name)
        return pltpu.make_async_remote_copy(
            src, dst, q.at[stage, 0], q.at[stage, 1], device_id=(clip_at, tm_at), device_id_type=MESH
        )

    def stage_ref(p, stage):
        part = getattr(r, ("gc_", "g1_", "g2_", "g3_", "g4_")[stage] + p.name)
        return part if stage < 3 else part.at[pl.ds(0, part.shape[0] - 1)]

    def stage_wait(p, stage, which):
        part = stage_ref(p, stage)
        pltpu.make_async_copy(part, part, getattr(r, "gs_" + p.name).at[stage, which]).wait()

    def add(dst, src):
        dst[...] = (dst[...].astype(F32) + src[...].astype(F32)).astype(BF16)

    def stage0(p):
        land = getattr(r, "gc_" + p.name)
        for z in range(d.nz):
            stage_copy(p, 0, block(p, 2 * z + 1 - core), land.at[z], clip, tm + 1 - 2 * core).start()

    def stage1(p):
        stage_wait(p, 0, 1)
        here, land = getattr(r, "gc_" + p.name), getattr(r, "g1_" + p.name)
        for z in range(d.nz):
            add(here.at[z], block(p, 2 * z + core))
        b = bits(p)[0]
        src = here.at[(slice(None),) + p.window(1, 1 - b)]
        stage_copy(p, 1, src, land, clip + step[p.first], tm).start()

    def stage2(p):
        stage_wait(p, 1, 1)
        before, here, land = (getattr(r, q + p.name) for q in ("gc_", "g1_", "g2_"))
        b = bits(p)
        for z in range(d.nz):
            add(here.at[z], before.at[(z,) + p.window(1, b[0])])
        src = here.at[(slice(None),) + p.window(2, 1 - b[1])]
        stage_copy(p, 2, src, land, clip + step["y" if p.first == "x" else "x"], tm).start()

    def stage3(p):
        stage_wait(p, 2, 1)
        before, here, land = (getattr(r, q + p.name) for q in ("g1_", "g2_", "g3_"))
        b = bits(p)
        for z in range(d.nz):
            add(here.at[z], before.at[(z,) + p.window(2, b[1])])
        for k in range(1, d.nz):
            z = lax.rem(zed + k, d.nz)
            stage_copy(p, 3, here.at[z], land.at[zed], clip, 2 * z + core).start()
        land[zed] = here[zed]

    def stage4(p):
        stage_wait(p, 3, 1)
        here, land = getattr(r, "g3_" + p.name), getattr(r, "g4_" + p.name)
        land[clip] = jnp.sum(here[...].astype(F32), axis=0).astype(BF16)
        for k in range(1, d.nc):
            at = lax.rem(clip + k, d.nc)
            stage_copy(p, 4, land.at[clip], land.at[clip], at, tm).start()

    slab = dict(sb0=(0, 0), sb1=(2, 0), wb=(0, 128), nb=(4, 0), mb=(5, 0), wa=(6, 0), na=(5, 64), ma=(7, 64))

    def out_copies(p):
        j, row = slab[p.name]
        out = getattr(r, "o_" + p.weight)
        wide = min(p.n, d.cb)
        i = [q.name for q in d.pieces].index(p.name)
        return [
            pltpu.make_async_copy(
                r.b3s.at[j + c, row : row + p.rb, :wide],
                out.at[:, p.lo + c * wide : p.lo + (c + 1) * wide],
                r.gsem.at[i, c],
            )
            for c in range(p.n // wide)
        ]

    def stage5(p):
        stage_wait(p, 4, 1)
        land = getattr(r, "g4_" + p.name)
        j, row = slab[p.name]
        rows, cols = p.shape2
        for q in range(d.nc):
            b = (q % 2, q // 2) if p.first == "x" else (q // 2, q % 2)
            at = [0, 0]
            size = [p.rb, p.n]
            for axis, one_bit in zip(p.split, b):
                k = 0 if axis == "r" else 1
                size[k] //= 2
                at[k] += one_bit * size[k]
            for lo in range(0, cols, min(cols, d.cb)):
                col = at[1] + lo
                r.b3s[
                    j + col // d.cb, row + at[0] : row + at[0] + rows,
                    col % d.cb : col % d.cb + min(cols, d.cb),
                ] = land[q, :, lo : lo + min(cols, d.cb)].astype(F32)
        for copy in out_copies(p):
            copy.start()

    named = {p.name: p for p in d.pieces}
    stages = (stage0, stage1, stage2, stage3, stage4, stage5)

    def send(stage, *pieces):
        for name in pieces:
            if d.staged:
                stages[stage](named[name])

    def halo_source(i, side):
        src = getattr(r, HALO[i][0])
        if HALO[i][0] == "dz2":
            return src.at[2 * side : 2 * side + 2, d.r2 // 2 :, :]
        if HALO[i][0] == "dva":
            return src.at[side * d.n : (side + 1) * d.n]
        return src.at[side]

    def halo_target(i, side):
        dst = getattr(r, HALO[i][1])
        if HALO[i][1] == "dva":
            return dst.at[(2 + side) * d.n : (3 + side) * d.n]
        return dst.at[side]

    def halo_copy(i, side):
        return pltpu.make_async_remote_copy(
            halo_source(i, side), halo_target(i, 1 - side), r.hsend.at[i, side], r.hrecv.at[i, 1 - side],
            device_id=(clip, tm + (2 * side - 1)), device_id_type=MESH,
        )

    def halo_start(i):
        @pl.when(tm > 0)
        def _():
            halo_copy(i, 0).start()

        @pl.when(tm < d.nt - 1)
        def _():
            halo_copy(i, 1).start()

    def halo_wait(i):
        lower, upper = halo_target(i, 0), halo_target(i, 1)

        @pl.when(tm > 0)
        def _():
            pltpu.make_async_copy(lower, lower, r.hrecv.at[i, 0]).wait()

        @pl.when(tm < d.nt - 1)
        def _():
            pltpu.make_async_copy(upper, upper, r.hrecv.at[i, 1]).wait()

        @pl.when(tm == 0)
        def _():
            lower[...] = jnp.zeros(lower.shape, lower.dtype)

        @pl.when(tm == d.nt - 1)
        def _():
            upper[...] = jnp.zeros(upper.shape, upper.dtype)

    def halo_drain(i):
        @pl.when(tm > 0)
        def _():
            pltpu.make_async_copy(
                halo_source(i, 0), halo_source(i, 0), r.hsend.at[i, 0]
            ).wait()

        @pl.when(tm < d.nt - 1)
        def _():
            pltpu.make_async_copy(
                halo_source(i, 1), halo_source(i, 1), r.hsend.at[i, 1]
            ).wait()

    order = {name: i for i, name in enumerate(NORMS)}
    width = dict(na=d.ca, da=d.ca, wa=d.c0, nb=d.cb, db=d.cb, wb=d.co, sb=d.co)

    def norm_set(name, sums, scale):
        i, c = order[name], width[name]
        inv = r.inv[:, :c] * scale
        mu = sums[0] * inv
        rs = lax.rsqrt(sums[1] * inv - mu * mu + epsilon)
        s = r.vec[2 * i : 2 * i + 1, :c] * rs
        r.par[i, 0:1, :c] = s
        r.par[i, 1:2, :c] = r.vec[2 * i + 1 : 2 * i + 2, :c] - mu * s
        r.par[i, 2:3, :c] = rs
        r.par[i, 3:4, :c] = mu

    def norm_of(name, lo, hi):
        i = order[name]
        return r.par[i, 0:1, lo:hi], r.par[i, 1:2, lo:hi]

    def back_set(name, sum_one, sum_two, scale):
        i, c = order[name], width[name]
        inv = r.inv[:, :c] * scale
        s, rs, mu = r.par[i, 0:1, :c], r.par[i, 2:3, :c], r.par[i, 3:4, :c]
        dgain = rs * (sum_two - mu * sum_one)
        gamma = s * rs * dgain * inv
        r.par[i, 4:5, :c] = s * sum_one * inv - gamma * mu
        r.par[i, 5:6, :c] = gamma
        r.small[2 * i : 2 * i + 1, :c] = dgain
        r.small[2 * i + 1 : 2 * i + 2, :c] = sum_one

    def back_of(name, lo, hi):
        i = order[name]
        return r.par[i, 0:1, lo:hi], r.par[i, 4:5, lo:hi], r.par[i, 5:6, lo:hi]

    def acc_clear(k, c):
        for i in range(k):
            r.acc[i, :, :c] = jnp.zeros((8, c), F32)

    def acc_rows(k, c):
        return [jnp.sum(r.acc[i, :, :c], axis=0, keepdims=True) for i in range(k)]

    def lanes(c, step=LANES):
        return [(lo, lo + step) for lo in range(0, c, step)]

    def slot_of(f):
        n = f // d.t
        return n * d.slots + 1 + (f - n * d.t)

    acc_clear(2, d.ca)
    weight_copy(0).wait()

    @pl.loop(0, d.f)
    def _(f):
        frame_copy(f).wait()
        v = dot(r.x[f], r.w_na[...])
        r.a1[f] = v.astype(BF16)
        m = mask_f(f)
        r.acc[0, :, : d.ca] += rows8(v) * m
        r.acc[1, :, : d.ca] += rows8(v * v) * m

    for n in range(d.n):
        r.dva[n] = r.a1[n * d.t]
        r.dva[d.n + n] = r.a1[n * d.t + frames - 1]
    pl.semaphore_wait(barrier, sum(size - 1 for _, _, size in d.phases))
    cells = (jnp.minimum(live, d.n) * frames * (d.h * d.w)).astype(F32)
    ar_start("na", acc_rows(2, d.ca) + [jnp.full((1, d.ca), 1.0, F32) * cells])
    halo_start(0)
    for i in range(3):
        src, dst = ((r.i_kta, r.kta), (r.i_ktb, r.ktb), (r.i_vec, r.vec))[i]
        pltpu.make_async_copy(src, dst, r.wsem.at[8 + i]).wait()
    for ref in (r.v1, r.v2):
        @pl.loop(0, d.n * d.slots)
        def _(i):
            zero = jnp.zeros((d.wp, ref.shape[2]), ref.dtype)
            ref[i, 0 : d.wp, :] = zero
            ref[i, d.er - d.wp : d.er, :] = zero
    weight_copy(1).wait()
    ar_mid("na")
    sums = ar_end("na")
    inv_cells = 1.0 / sums[2]
    for lo, hi in lanes(d.co, d.ca):
        r.inv[:, lo:hi] = inv_cells
    norm_set("na", sums, 1.0)

    half = float((d.h * d.w * 2) // (d.h2 * d.w2))

    def activated(v, name, lo, hi, cols, m):
        s, b = norm_of(name, lo, hi)
        return silu(v * s + b) * (cols * m)

    def mixed(hidden, weight):
        return dot(hidden, weight).astype(BF16)

    def inner(ref_in, hid, framed, name, weight, c, half_i):
        cols = full_cols

        @pl.loop(0, d.f)
        def _(f):
            m = mask_f(f)
            for lo, hi in lanes(c):
                hid[f, :, lo:hi] = activated(ref_in[f, :, lo:hi].astype(F32), name, lo, hi, cols, m).astype(BF16)
            framed[slot_of(f), d.wp : d.wp + d.fr, :] = mixed(hid[f], weight[...]).astype(framed.dtype)

        halo_wait(half_i)
        sides = (halo_target(half_i, 0), halo_target(half_i, 1))
        for n in range(d.n):
            for side in range(2):
                m = (has_prev, has_next)[side] * one(n < live)
                h = jnp.concatenate(
                    [
                        activated(sides[side][n, :, lo:hi].astype(F32), name, lo, hi, cols, m).astype(BF16)
                        for lo, hi in lanes(c)
                    ],
                    axis=1,
                )
                v = mixed(h, weight[...])
                if side == 0:
                    framed[n * d.slots, d.wp : d.wp + d.fr, :] = v.astype(framed.dtype)
                else:
                    for k in range(1, d.t):
                        at = (n * d.slots + 1 + k, slice(d.wp, d.wp + d.fr), slice(None))
                        framed[at] = (framed[at].astype(F32) + v.astype(F32) * one(frames == k)).astype(
                            framed.dtype
                        )
                    framed[n * d.slots + 1 + d.t, d.wp : d.wp + d.fr, :] = v.astype(framed.dtype)

    inner(r.a1, r.h1, r.v1, "na", r.w_ma, d.ca, 0)

    def taps(ref, lo):
        return [ref[i : i + 1, lo : lo + LANES] for i in range(27)]

    acc_clear(2, d.ca)

    @pl.loop(0, d.f)
    def _(f):
        base = slot_of(f) - 1
        m = mask_f(f)
        for lo, hi in lanes(d.ca):
            k = taps(r.kta, lo)
            one_sum = jnp.zeros((8, LANES), F32)
            two_sum = jnp.zeros((8, LANES), F32)
            for h in range(d.h):
                parts = [None] * 3
                for a in range(3):
                    for b in range(3):
                        v = r.v1[base + a, (h + b) * d.wp : (h + b + 1) * d.wp, lo:hi].astype(F32)
                        for e in range(3):
                            p = v * k[9 * a + 3 * b + e]
                            parts[e] = p if parts[e] is None else parts[e] + p
                o = parts[1] + pltpu.roll(parts[0], 1, 0) + pltpu.roll(parts[2], d.wp - 1, 0)
                o = o * row_cols
                r.d1[f, h * d.wp : (h + 1) * d.wp, lo:hi] = o
                one_sum += rows8(o)
                two_sum += rows8(o * o)
            r.acc[0, :, lo:hi] += one_sum * m
            r.acc[1, :, lo:hi] += two_sum * m

    ar_start("da", acc_rows(2, d.ca))
    weight_copy(2).wait()
    ar_mid("da")
    norm_set("da", ar_end("da"), 1.0)

    acc_clear(2, d.c0)

    @pl.loop(0, d.f)
    def _(f):
        m = mask_f(f)
        for lo, hi in lanes(d.ca):
            r.h2[f, :, lo:hi] = activated(r.d1[f, :, lo:hi], "da", lo, hi, full_cols, m).astype(BF16)
        for lo, hi in lanes(d.c0, 256):
            v = dot(r.h2[f], r.w_wa[:, lo:hi])
            r.a3[f, :, lo:hi] = v.astype(BF16)
            r.acc[0, :, lo:hi] += rows8(v)
            r.acc[1, :, lo:hi] += rows8(v * v)

    ar_start("wa", acc_rows(2, d.c0))
    weight_copy(3).wait()
    ar_mid("wa")
    norm_set("wa", ar_end("wa"), 1.0)

    def joined(f, lo, hi):
        s, b = norm_of("wa", lo, hi)
        x = r.x[f, :, lo:hi].astype(F32)
        return r.a3[f, :, lo:hi].astype(F32) * s + b + x

    acc_clear(2, d.cb)

    @pl.loop(0, d.f)
    def _(f):
        m = mask_f(f)
        for lo, hi in lanes(d.c0):
            r.y1[f, :, lo:hi] = (silu(joined(f, lo, hi)) * (full_cols * m)).astype(BF16)
        for lo, hi in lanes(d.cb, 256):
            v = dot(r.y1[f], r.w_nb[:, lo:hi])
            r.b1[f, :, lo:hi] = v.astype(BF16)
            r.acc[0, :, lo:hi] += rows8(v)
            r.acc[1, :, lo:hi] += rows8(v * v)

    for n in range(d.n):
        r.hs2[0, n] = r.b1[n * d.t]
        r.hs2[1, n] = r.b1[n * d.t + frames - 1]
    ar_start("nb", acc_rows(2, d.cb))
    halo_start(1)

    rows_e = lax.broadcasted_iota(jnp.int32, (d.hr, d.fr), 0)
    cols_e = lax.broadcasted_iota(jnp.int32, (d.hr, d.fr), 1)
    pick = one(
        (cols_e == (rows_e // d.wh) * (2 * d.wp) + lax.rem(rows_e, d.wh) * 2)
    ).astype(BF16)

    @pl.loop(0, d.f2)
    def _(i):
        n = i // d.t2
        f = n * d.t + parity + 2 * (i - n * d.t2)
        for lo, hi in lanes(d.c0, 512):
            r.e[i, :, lo:hi] = dot(pick, r.y1[f, :, lo:hi])

    r.eb[...] = r.e[...].reshape(d.r2, d.c0).astype(BF16)
    weight_copy(6).wait()
    acc_clear(2, d.co)

    @pl.loop(0, d.co // d.cb)
    def _(j):
        for half_lo in range(0, d.cb, 256):
            at = pl.ds(pl.multiple_of(j * d.cb + half_lo, 256), 256)
            v = dot(r.eb[...], r.w_sb[:, at])
            r.b3s[d.co // d.cb + j, :, half_lo : half_lo + 256] = v
            r.acc[0, :, at] += rows8(v)
            r.acc[1, :, at] += rows8(v * v)

    ar_start("sk", acc_rows(2, d.co))
    weight_copy(4).wait()
    ar_mid("nb")
    norm_set("nb", ar_end("nb"), 1.0)

    inner(r.b1, r.g1, r.v2, "nb", r.w_mb, d.cb, 1)

    @pl.loop(0, d.f2)
    def _(i):
        n = i // d.t2
        base = n * d.slots + parity + 2 * (i - n * d.t2)
        for lo, hi in lanes(d.cb):
            k = taps(r.ktb, lo)
            for h in range(d.h2):
                parts = [None] * 3
                for a in range(3):
                    for b in range(3):
                        at = (2 * h + b) * d.wp
                        v = r.v2[base + a, at : at + d.wp, lo:hi].astype(F32)
                        for e in range(3):
                            p = v * k[9 * a + 3 * b + e]
                            parts[e] = p if parts[e] is None else parts[e] + p
                o = parts[1] + pltpu.roll(parts[0], 1, 0) + pltpu.roll(parts[2], d.wp - 1, 0)
                r.dz2[i, h * d.wp : (h + 1) * d.wp, lo:hi] = o

    hw = d.h2 * d.wp
    thin = one(
        lax.broadcasted_iota(jnp.int32, (d.hr, hw), 1)
        == 2 * lax.broadcasted_iota(jnp.int32, (d.hr, hw), 0)
    ).astype(BF16)

    def split(v):
        high = v.astype(BF16)
        rest = v - high.astype(F32)
        mid = rest.astype(BF16)
        return high, mid, (rest - mid.astype(F32)).astype(BF16)

    acc_clear(2, d.cb)

    @pl.loop(0, d.f2)
    def _(i):
        m = mask_o(i)
        for lo, hi in lanes(d.cb):
            v = sum(dot(thin, p) for p in split(r.dz2[i, :hw, lo:hi])) * half_cols
            r.d2[i, :, lo:hi] = v
            r.acc[0, :, lo:hi] += rows8(v) * m
            r.acc[1, :, lo:hi] += rows8(v * v) * m

    ar_start("db", acc_rows(2, d.cb))
    ar_mid("sk")
    weight_copy(5).wait()
    ar_mid("db")
    norm_set("sb", ar_end("sk"), half)
    norm_set("db", ar_end("db"), half)

    def d2_rows(ref, i, lo, hi):
        return ref[i, :, lo:hi]

    for i in range(d.f2):
        m = mask_o(i)
        for lo, hi in lanes(d.cb):
            g = activated(d2_rows(r.d2, i, lo, hi), "db", lo, hi, half_cols, m)
            r.e[i, :, lo:hi] = g
    r.g2[...] = r.e[:, :, : d.cb].reshape(d.r2, d.cb).astype(BF16)
    acc_clear(2, d.co)

    @pl.loop(0, d.co // d.cb)
    def _(j):
        for half_lo in range(0, d.cb, 256):
            at = pl.ds(pl.multiple_of(j * d.cb + half_lo, 256), 256)
            v = dot(r.g2[...], r.w_wb[:, at])
            r.b3s[j, :, half_lo : half_lo + 256] = v
            r.acc[0, :, at] += rows8(v)
            r.acc[1, :, at] += rows8(v * v)

    ar_start("wb", acc_rows(2, d.co))
    pltpu.make_async_copy(r.cotangent, r.ds, r.wsem.at[11]).wait()
    half_all = jnp.concatenate(
        [half_cols * mask_o(jnp.int32(i)) for i in range(d.f2)], axis=0
    )
    ar_mid("wb")
    norm_set("wb", ar_end("wb"), half)

    acc_clear(3, d.co)

    @pl.loop(0, d.co // LANES)
    def _(q):
        per = d.cb // LANES
        j = q // per
        at = pl.ds(pl.multiple_of((q - j * per) * LANES, LANES), LANES)
        lane = pl.ds(pl.multiple_of(q * LANES, LANES), LANES)
        i3, isk = order["wb"], order["sb"]
        b3, s = r.b3s[j, :, at], r.b3s[d.co // d.cb + j, :, at]
        z = b3 * r.par[i3, 0:1, lane] + r.par[i3, 1:2, lane]
        z = z + s * r.par[isk, 0:1, lane] + r.par[isk, 1:2, lane]
        g = logistic(z)
        r.db3[:, lane] = (z * g * half_all).astype(BF16)
        sl = g * (1.0 + z * (1.0 - g)) * half_all
        dz = r.ds[:, lane].astype(F32) * sl
        r.dz2[j, :, at] = dz
        r.acc[0, :, lane] += rows8(dz)
        r.acc[1, :, lane] += rows8(dz * b3)
        r.acc[2, :, lane] += rows8(dz * s)

    out_copy = pltpu.make_async_copy(r.db3, r.block_out, r.osem.at[0])
    out_copy.start()
    ar_start("gz", acc_rows(3, d.co))
    ar_mid("gz")
    sums = ar_end("gz")
    back_set("wb", sums[0], sums[1], half)
    back_set("sb", sums[0], sums[2], half)

    out_copy.wait()
    for lo in range(0, d.co, LANES):
        j, at = lo // d.cb, lo % d.cb
        dz = r.dz2[j, :, at : at + LANES]
        for name, off, dst in (("wb", 0, r.db3), ("sb", d.co // d.cb, r.ds)):
            al, be, ga = back_of(name, lo, lo + LANES)
            v = (dz * al - be - r.b3s[off + j, :, at : at + LANES] * ga) * half_all
            dst[:, lo : lo + LANES] = v.astype(BF16)

    acc_clear(2, d.cb)
    for lo, hi in lanes(d.cb, 256):
        g = dot_bt(r.db3[...], r.w_wb[lo:hi, :])
        for i in range(d.f2):
            s, b = norm_of("db", lo, hi)
            v = r.d2[i, :, lo:hi]
            dn = g[i * d.hr : (i + 1) * d.hr, :] * slope(v * s + b)
            r.dz2[i, : d.hr, lo:hi] = dn
            r.acc[0, :, lo:hi] += rows8(dn)
            r.acc[1, :, lo:hi] += rows8(dn * v)
    for n in range(d.n):
        for side, j in ((0, 0), (1, out_frames - 1)):
            at = d.r2 // 2 + n * d.hr
            r.dz2[2 * side, at : at + d.hr, :] = r.dz2[n * d.t2 + j, : d.hr, :]
            r.dz2[2 * side + 1, at : at + d.hr, :] = r.d2[n * d.t2 + j]
    ar_start("gdb", acc_rows(2, d.cb))
    halo_start(2)

    def weight_grad(name, x, y, step, lo=0, hi=None):
        w = getattr(r, "w_" + name)
        for at in range(lo, hi or w.shape[1], step):
            w[:, at : at + step] = dot_at(x, y(at, at + step)).astype(BF16)

    for lo, hi in lanes(d.c0, 256):
        v = dot_bt(r.ds[...], r.w_sb[lo:hi, :])
        for i in range(d.f2):
            r.e[i, :, lo:hi] = v[i * d.hr : (i + 1) * d.hr, :]
    weight_grad("wb", r.g2[...], lambda lo, hi: r.db3[:, lo:hi], 512)
    send(0, "wb")
    ar_mid("gdb")
    weight_grad("sb", r.eb[...], lambda lo, hi: r.ds[:, lo:hi], 256, 0, d.co // 2)
    send(0, "sb0")
    weight_grad("sb", r.eb[...], lambda lo, hi: r.ds[:, lo:hi], 256, d.co // 2, d.co)
    send(0, "sb1")
    back_set("db", *ar_end("gdb"), half)

    per = d.ca // LANES
    spread = one(
        lax.broadcasted_iota(jnp.int32, (hw, d.hr), 0)
        == 2 * lax.broadcasted_iota(jnp.int32, (hw, d.hr), 1)
    ).astype(BF16)

    def u_at(slot, row, rows, lo):
        at = (lo // d.ca) * d.ur
        return (slot, slice(at + row, at + row + rows), slice(lo % d.ca, lo % d.ca + LANES))

    @pl.loop(0, d.n * d.slots)
    def _(i):
        r.u[i] = jnp.zeros((d.er, d.ca), F32)

    def grad_d2(dn, v, lo, m):
        al, be, ga = back_of("db", lo, lo + LANES)
        g = (dn * al - be - v * ga) * (half_cols * m)
        return sum(dot(spread, p) for p in split(g))

    halo_wait(2)
    for n in range(d.n):
        for lo in range(0, d.cb, LANES):
            own = [
                grad_d2(r.dz2[n * d.t2 + j, : d.hr, lo : lo + LANES], r.d2[n * d.t2 + j, :, lo : lo + LANES],
                        lo, mask_o(jnp.int32(n * d.t2 + j)))
                for j in range(d.t2)
            ]
            before = grad_d2(
                r.hr3[0, 0, n * d.hr : (n + 1) * d.hr, lo : lo + LANES], r.hr3[0, 1, n * d.hr : (n + 1) * d.hr, lo : lo + LANES], lo,
                has_prev * one(n < live) * one(parity == 1),
            )
            after = grad_d2(
                r.hr3[1, 0, n * d.hr : (n + 1) * d.hr, lo : lo + LANES], r.hr3[1, 1, n * d.hr : (n + 1) * d.hr, lo : lo + LANES], lo,
                has_next * one(n < live) * one(((start + frames) & 1) == 0),
            )
            base = n * d.slots
            r.u[u_at(base, 0, hw, lo)] = before
            for i in range(1, d.t + 2):
                v = jnp.zeros((hw, LANES), F32)
                for j in range(d.t2):
                    p = i - 1 - 2 * j
                    if p in (0, 1):
                        v = v + own[j] * one(parity == p)
                if i >= 3:
                    v = v + after * one(frames + 1 == i)
                r.u[u_at(base + i, 0, hw, lo)] = v

    acc_clear(2, d.cb)

    @pl.loop(0, d.f)
    def _(f):
        base = slot_of(f)
        m = mask_f(f)
        for lo, hi in lanes(d.cb):
            k = taps(r.ktb, lo)
            for h in range(d.h):
                rows = ((h // 2, 1),) if h % 2 == 0 else ((h // 2 + 1, 0), (h // 2, 2))
                parts = [None] * 3
                for a in range(3):
                    for row, b in rows:
                        if row >= d.h2:
                            continue
                        v = r.u[u_at(base + 1 - a, row * d.wp, d.wp, lo)]
                        for e in range(3):
                            p = v * k[9 * a + 3 * b + e]
                            parts[e] = p if parts[e] is None else parts[e] + p
                o = parts[1] + pltpu.roll(parts[0], d.wp - 1, 0) + pltpu.roll(parts[2], 1, 0)
                r.dvb[f, h * d.wp : (h + 1) * d.wp, lo:hi] = o.astype(BF16)
        for lo, hi in lanes(d.cb, 256):
            g = dot_bt(r.dvb[f], r.w_mb[lo:hi, :])
            for at in range(lo, hi, LANES):
                s, b = norm_of("nb", at, at + LANES)
                v = r.b1[f, :, at : at + LANES].astype(F32)
                dn = g[:, at - lo : at - lo + LANES] * slope(v * s + b) * (full_cols * m)
                r.b3s[f, :, at : at + LANES] = dn
                r.acc[0, :, at : at + LANES] += rows8(dn)
                r.acc[1, :, at : at + LANES] += rows8(dn * v)

    ar_start("gnb", acc_rows(2, d.cb))
    send(1, "wb", "sb0", "sb1")

    def shifted(v):
        return (pltpu.roll(v, d.wp - 1, 0), v, pltpu.roll(v, 1, 0))

    for lo in range(0, d.cb, LANES):
        def body(i, sums):
            n = i // d.t2
            slot = n * d.slots + parity + 2 * (i - n * d.t2)
            sums = list(sums)
            for h in range(d.h2):
                g = shifted(r.u[u_at(slot + 1, h * d.wp, d.wp, lo)] * mask_o(i))
                for a in range(3):
                    for b in range(3):
                        at = (2 * h + b) * d.wp
                        v = r.v2[slot + a, at : at + d.wp, lo : lo + LANES].astype(F32)
                        for e in range(3):
                            sums[9 * a + 3 * b + e] += rows8(v * g[e])
            return tuple(sums)

        sums = lax.fori_loop(0, d.f2, body, (jnp.zeros((8, LANES), F32),) * 27)
        for i in range(27):
            r.gkb[i : i + 1, lo : lo + LANES] = jnp.sum(sums[i], axis=0, keepdims=True)

    def flat(ref):
        return ref[...].reshape(d.f * d.fr, ref.shape[-1])

    ar_start("kb", [r.gkb[...]])
    ar_mid("gnb")
    weight_grad("mb", flat(r.g1), lambda lo, hi: r.dvb[:, :, lo:hi].reshape(d.f * d.fr, hi - lo), 256)
    send(0, "mb")
    back_set("nb", *ar_end("gnb"), 1.0)

    acc_clear(2, d.c0)

    @pl.loop(0, d.f)
    def _(f):
        m = mask_f(f)
        n = f // d.t
        t = f - n * d.t
        for lo, hi in lanes(d.cb):
            al, be, ga = back_of("nb", lo, hi)
            v = (r.b3s[f, :, lo:hi] * al - be - r.b1[f, :, lo:hi].astype(F32) * ga) * (full_cols * m)
            r.dvb[f, :, lo:hi] = v.astype(BF16)

    for i in range(0, d.c0, d.er):
        for lo, hi in lanes(d.cb, 256):
            x = r.y1[:, :, i : i + d.er].reshape(d.f * d.fr, d.er)
            y = r.dvb[:, :, lo:hi].reshape(d.f * d.fr, hi - lo)
            r.v2[i // d.er, :, lo:hi] = dot_at(x, y).astype(BF16)
    send(0, "nb")

    @pl.loop(0, d.f)
    def _(f):
        m = mask_f(f)
        n = f // d.t
        t = f - n * d.t
        j = jnp.clip((t - parity) // 2, 0, d.t2 - 1)
        flag = one(((t - parity) & 1) == 0)
        for lo, hi in lanes(d.c0, 256):
            g = dot_bt(r.dvb[f], r.w_nb[lo:hi, :])
            for at in range(lo, hi, LANES):
                parts = split(r.e[n * d.t2 + j, :, at : at + LANES] * flag)
                up = sum(dot_at(pick, p) for p in parts[:2])
                z = joined(f, at, at + LANES)
                dz = (g[:, at - lo : at - lo + LANES] + up) * slope(z) * (full_cols * m)
                r.y1[f, :, at : at + LANES] = dz.astype(BF16)
                v = r.a3[f, :, at : at + LANES].astype(F32)
                r.acc[0, :, at : at + LANES] += rows8(dz)
                r.acc[1, :, at : at + LANES] += rows8(dz * v)

    ar_start("gwa", acc_rows(2, d.c0))
    send(2, "wb", "sb0", "sb1")
    ar_mid("kb")
    ar_mid("gwa")
    send(1, "mb", "nb")
    back_set("wa", *ar_end("gwa"), 1.0)

    acc_clear(2, d.ca)

    @pl.loop(0, d.f)
    def _(f):
        m = mask_f(f)
        for lo, hi in lanes(d.c0):
            al, be, ga = back_of("wa", lo, hi)
            v = r.y1[f, :, lo:hi].astype(F32) * al - be - r.a3[f, :, lo:hi].astype(F32) * ga
            r.a3[f, :, lo:hi] = (v * (full_cols * m)).astype(BF16)
        g = dot_bt(r.a3[f], r.w_wa[...])
        for lo, hi in lanes(d.ca):
            s, b = norm_of("da", lo, hi)
            v = r.d1[f, :, lo:hi]
            dn = g[:, lo:hi] * slope(v * s + b)
            r.u[slot_of(f), d.wp : d.wp + d.fr, lo:hi] = dn
            r.acc[0, :, lo:hi] += rows8(dn)
            r.acc[1, :, lo:hi] += rows8(dn * v)

    halo_drain(1)
    for n in range(d.n):
        for side, k in ((0, 0), (1, frames - 1)):
            r.hs2[side, n, :, : d.ca] = r.u[n * d.slots + 1 + k, d.wp : d.wp + d.fr, :].astype(BF16)
            r.hs2[side, n, :, d.ca :] = r.d1[n * d.t + k].astype(BF16)
    ar_start("gda", acc_rows(2, d.ca))
    halo_start(3)
    send(3, "wb", "sb0", "sb1")
    ar_mid("gda")
    send(2, "mb", "nb")
    weight_grad("wa", flat(r.h2), lambda lo, hi: r.a3[:, :, lo:hi].reshape(d.f * d.fr, hi - lo), 256)
    send(0, "wa")

    @pl.loop(0, d.n * d.slots)
    def _(i):
        zero = jnp.zeros((d.wp, d.ca), F32)
        r.u[i, 0 : d.wp, :] = zero
        r.u[i, d.er - d.wp : d.er, :] = zero

    back_set("da", *ar_end("gda"), 1.0)

    def grad_d1(dn, v, lo, hi, m):
        al, be, ga = back_of("da", lo, hi)
        return (dn * al - be - v * ga) * (full_cols * m)

    mid_rows = slice(d.wp, d.wp + d.fr)

    @pl.loop(0, d.f)
    def _(f):
        m = mask_f(f)
        for lo, hi in lanes(d.ca):
            r.u[slot_of(f), mid_rows, lo:hi] = grad_d1(
                r.u[slot_of(f), mid_rows, lo:hi], r.d1[f, :, lo:hi], lo, hi, m
            )

    halo_wait(3)
    for n in range(d.n):
        for lo, hi in lanes(d.ca):
            r.u[n * d.slots, mid_rows, lo:hi] = grad_d1(
                r.hr2[0, n, :, lo:hi].astype(F32), r.hr2[0, n, :, d.ca + lo : d.ca + hi].astype(F32), lo, hi,
                has_prev * one(n < live),
            )
            v = grad_d1(
                r.hr2[1, n, :, lo:hi].astype(F32), r.hr2[1, n, :, d.ca + lo : d.ca + hi].astype(F32), lo, hi,
                has_next * one(n < live),
            )
            for k in range(1, d.t):
                at = n * d.slots + 1 + k
                r.u[at, mid_rows, lo:hi] = r.u[at, mid_rows, lo:hi] + v * one(frames == k)
            r.u[n * d.slots + 1 + d.t, mid_rows, lo:hi] = v

    halo_drain(0)
    acc_clear(2, d.ca)

    @pl.loop(0, d.f)
    def _(f):
        base = slot_of(f)
        m = mask_f(f)
        for lo, hi in lanes(d.ca):
            k = taps(r.kta, lo)
            for h in range(d.h):
                parts = [None] * 3
                for a in range(3):
                    for b in range(3):
                        v = r.u[base + 1 - a, (h + 2 - b) * d.wp : (h + 3 - b) * d.wp, lo:hi]
                        for e in range(3):
                            p = v * k[9 * a + 3 * b + e]
                            parts[e] = p if parts[e] is None else parts[e] + p
                o = parts[1] + pltpu.roll(parts[0], d.wp - 1, 0) + pltpu.roll(parts[2], 1, 0)
                r.dva[f, h * d.wp : (h + 1) * d.wp, lo:hi] = o.astype(BF16)
        g = dot_bt(r.dva[f], r.w_ma[...])
        for lo, hi in lanes(d.ca):
            s, b = norm_of("na", lo, hi)
            v = r.a1[f, :, lo:hi].astype(F32)
            dn = g[:, lo:hi] * slope(v * s + b) * (full_cols * m)
            r.d1[f, :, lo:hi] = dn
            r.acc[0, :, lo:hi] += rows8(dn)
            r.acc[1, :, lo:hi] += rows8(dn * v)

    ar_start("gna", acc_rows(2, d.ca))
    send(4, "wb", "sb0", "sb1")
    send(3, "mb", "nb")
    send(1, "wa")

    for lo in range(0, d.ca, LANES):
        def body(f, sums):
            slot = slot_of(f)
            m = mask_f(f)
            sums = list(sums)
            for h in range(d.h):
                g = shifted(r.u[slot, (h + 1) * d.wp : (h + 2) * d.wp, lo : lo + LANES] * m)
                for a in range(3):
                    for b in range(3):
                        at = (h + b) * d.wp
                        v = r.v1[slot - 1 + a, at : at + d.wp, lo : lo + LANES].astype(F32)
                        for e in range(3):
                            sums[9 * a + 3 * b + e] += rows8(v * g[e])
            return tuple(sums)

        sums = lax.fori_loop(0, d.f, body, (jnp.zeros((8, LANES), F32),) * 27)
        for i in range(27):
            r.gka[i : i + 1, lo : lo + LANES] = jnp.sum(sums[i], axis=0, keepdims=True)

    ar_start("ka", [r.gka[...]])
    ar_mid("gna")
    weight_grad("ma", flat(r.h1), lambda lo, hi: r.dva[: d.f, :, lo:hi].reshape(d.f * d.fr, hi - lo), 256)
    send(0, "ma")
    back_set("na", *ar_end("gna"), 1.0)

    def grad_copy(f):
        return pltpu.make_async_copy(r.y1.at[f], r.input_grad.at[f], r.isem.at[f])

    @pl.loop(0, d.f)
    def _(f):
        m = mask_f(f)
        for lo, hi in lanes(d.ca):
            al, be, ga = back_of("na", lo, hi)
            v = (r.d1[f, :, lo:hi] * al - be - r.a1[f, :, lo:hi].astype(F32) * ga) * (full_cols * m)
            r.dva[f, :, lo:hi] = v.astype(BF16)

    x = r.x[...].reshape(d.f * d.fr, d.c0)
    y = r.dva[: d.f].reshape(d.f * d.fr, d.ca)
    for i in range(0, d.c0, d.er):
        r.v1[i // d.er] = dot_at(x[:, i : i + d.er], y).astype(BF16)
    send(0, "na")
    send(2, "wa")
    send(4, "mb", "nb")
    send(1, "ma")
    send(5, "wb", "sb0", "sb1")
    ar_mid("ka")

    @pl.loop(0, d.f)
    def _(f):
        for lo, hi in lanes(d.c0, 256):
            g = dot_bt(r.dva[f], r.w_na[lo:hi, :]) + r.y1[f, :, lo:hi].astype(F32)
            r.y1[f, :, lo:hi] = g.astype(BF16)
        grad_copy(f).start()

    send(1, "na")
    send(3, "wa")
    send(2, "ma")
    send(5, "mb", "nb")
    send(2, "na")
    send(4, "wa")
    send(3, "ma")
    r.gka[...] = ar_end("ka")
    r.gkb[...] = ar_end("kb")
    tail = [(r.small, r.o_small), (r.gka, r.o_gka), (r.gkb, r.o_gkb)]
    send(3, "na")
    send(4, "ma")
    send(5, "wa")
    send(4, "na")
    send(5, "ma")
    send(5, "na")
    if not d.staged:
        tail += [(getattr(r, "w_" + n), getattr(r, "o_" + n)) for n in ("ma", "wa", "mb", "wb", "sb")]
        for ref, out, rows, cols in ((r.v1, r.o_na, d.c0, d.ca), (r.v2, r.o_nb, d.c0, d.cb)):
            for i in range(0, rows, d.er):
                tail.append((ref.at[i // d.er], out.at[i : i + d.er, :]))
    tail = [pltpu.make_async_copy(src, dst, r.osem.at[1 + i]) for i, (src, dst) in enumerate(tail)]
    for copy in tail:
        copy.start()

    for f in range(d.f):
        grad_copy(f).wait()
    for copy in tail:
        copy.wait()
    for p in d.pieces:
        for copy in out_copies(p):
            copy.wait()
        for stage in range(5):
            stage_wait(p, stage, 0)
    for name in msgs:
        ar_drain(name)
    for i in (2, 3):
        halo_drain(i)


def per_device(mesh, *args):
    (
        clip_in, cotangent, frame_count, clip_count, narrow_a, narrow_gain_a, narrow_bias_a, mixing_a,
        depthwise_a, depth_gain_a, depth_bias_a, widen_a, widen_gain_a, widen_bias_a, narrow_b,
        narrow_gain_b, narrow_bias_b, mixing_b, depthwise_b, depth_gain_b, depth_bias_b, widen_b,
        widen_gain_b, widen_bias_b, shortcut_b, shortcut_gain_b, shortcut_bias_b,
    ) = args
    d = Dims(mesh, clip_in.shape, cotangent.shape, narrow_a.shape[1], narrow_b.shape[1])
    vectors = (
        narrow_gain_a, narrow_bias_a, depth_gain_a, depth_bias_a, widen_gain_a, widen_bias_a,
        narrow_gain_b, narrow_bias_b, depth_gain_b, depth_bias_b, widen_gain_b, widen_bias_b,
        shortcut_gain_b, shortcut_bias_b,
    )
    packed = jnp.stack([jnp.pad(v, (0, d.co - v.shape[0])) for v in vectors] + [jnp.zeros((d.co,), F32)] * 2)

    def columns(v, width):
        return jnp.pad(v, ((0, 0),) * 3 + ((0, width - v.shape[3]), (0, 0)))

    def taps_of(k):
        return jnp.pad(k.astype(F32).T, ((0, 5), (0, 0)))

    scratch = scratch_of(d)
    names = INPUTS + OUTPUTS + tuple(scratch)
    def grad_shape(w):
        if d.staged:
            return jax.ShapeDtypeStruct((w.shape[0] // d.nt, w.shape[1]), F32)
        return jax.ShapeDtypeStruct(w.shape, BF16)

    shapes = dict(
        block_out=jax.ShapeDtypeStruct((d.r2, d.co), BF16),
        input_grad=jax.ShapeDtypeStruct((d.f, d.fr, d.c0), BF16),
        o_small=jax.ShapeDtypeStruct((16, d.co), F32),
        o_gka=jax.ShapeDtypeStruct((32, d.ca), F32),
        o_gkb=jax.ShapeDtypeStruct((32, d.cb), F32),
        o_na=grad_shape(narrow_a),
        o_ma=grad_shape(mixing_a),
        o_wa=grad_shape(widen_a),
        o_nb=grad_shape(narrow_b),
        o_mb=grad_shape(mixing_b),
        o_wb=grad_shape(widen_b),
        o_sb=grad_shape(shortcut_b),
    )
    anywhere = pl.BlockSpec(memory_space=pl.ANY)
    scalars = pl.BlockSpec(memory_space=pltpu.SMEM)
    outs = pl.pallas_call(
        functools.partial(kernel, d, names),
        out_shape=[shapes[name] for name in OUTPUTS],
        in_specs=[scalars if name.endswith("_count") else anywhere for name in INPUTS],
        out_specs=[anywhere] * len(OUTPUTS),
        scratch_shapes=list(scratch.values()),
        compiler_params=pltpu.CompilerParams(
            collective_id=0, has_side_effects=True, vmem_limit_bytes=65200 * 1024
        ),
    )(
        columns(clip_in, d.wp).reshape(d.f, d.fr, d.c0),
        columns(cotangent, d.wh).reshape(d.r2, d.co), frame_count, clip_count, narrow_a, mixing_a, widen_a, narrow_b, mixing_b,
        widen_b, shortcut_b, taps_of(depthwise_a), taps_of(depthwise_b), packed,
    )
    out = dict(zip(OUTPUTS, outs))

    def share(g):
        if d.staged:
            return g
        part = lax.psum_scatter(g.astype(BF16), "tm", scatter_dimension=0, tiled=True)
        return lax.psum(part, "clip").astype(F32)

    tm = lax.axis_index("tm")

    def share_taps(g):
        rows = g.shape[1] // d.nt
        return lax.dynamic_slice_in_dim(g[:27], tm * rows, rows, 1).T

    small = out["o_small"]
    grads = [small[i, : v.shape[0]] for i, v in enumerate(vectors)]
    return (
        out["block_out"].reshape(d.n, d.t2, d.h2, d.wh, d.co)[:, :, :, : d.w2],
        out["input_grad"].reshape(d.n, d.t, d.h, d.wp, d.c0)[:, :, :, : d.w],
        share(out["o_na"]), grads[0], grads[1], share(out["o_ma"]), share_taps(out["o_gka"]),
        grads[2], grads[3], share(out["o_wa"]), grads[4], grads[5],
        share(out["o_nb"]), grads[6], grads[7], share(out["o_mb"]), share_taps(out["o_gkb"]),
        grads[8], grads[9], share(out["o_wb"]), grads[10], grads[11],
        share(out["o_sb"]), grads[12], grads[13],
    )


def solution(mesh):
    data = P("clip", "tm", None, None, None)
    rows = P("tm", None)
    in_specs = (data, data, P(), P("clip")) + (P(),) * 23
    block = (rows, P(), P(), rows, rows, P(), P(), rows, P(), P())
    out_specs = (data, data) + block + block + (rows, P(), P())
    return jax.shard_map(
        functools.partial(per_device, mesh), mesh=mesh, in_specs=in_specs, out_specs=out_specs,
        check_vma=False,
    )
```
